1024 devices in a mesh: row: 64 (over x, z), col: 16 (over y, core).
Axes of the slice: x: 4, y: 8, z: 16, core: 2. Of those that a mesh axis runs over, the one named last changes fastest.
Arguments:
- table: float32 [131072, 256], P(('row', 'col')), may hold values from -3 to 3
- blocks: float32 [1024, 16, 128, 128], P(('row', 'col')), may hold values from 0 to 0.05
- block_ids: int32 [1024, 16], P(('row', 'col')), may hold values from 0 to 1023, as said below
- counts: int32 [1024], P(('row', 'col')), may hold values from 4 to 16, as said below
- users: int32 [1024, 64], P(('row', 'col')), may hold values from 0 to 127
- positives: int32 [1024, 64], P(('row', 'col')), may hold values from 0 to 127
- neg_index: int32 [1024, 64], P(('row', 'col')), may hold values from 0 to 63
- popular: int32 [1024, 64], P(('row', 'col')), may hold values from 0 to 127
Outputs:
- gradient: float32 [131072, 256], P(('row', 'col'))
- span_loss: float32 [1024], P(('row', 'col'))
The draws below stay inside these ranges and needn't reach their ends.
Inputs may be any that keep to these rules, and one draw needn't show every extreme that they name: `block_ids`: each row names 16 different positions rb * 64 + cb of one device's 16 x 64 grid of blocks. `counts`: some device has all 16 slots live.
All inputs are finite; a program needn't handle non-finite values.
Results may differ from the reference program's by a relative error of at most 0.0003.
Values sent between devices are 32-bit elements; how exact they have to be, the bound alone decides.
No kernel may reach another device: no remote copies, remote signals or barrier semaphores. Data moves between devices by JAX's collectives and lax.ppermute only.
A program may use at most 64 MiB of HBM per device.

```python
import math
from functools import partial
import jax
import jax.numpy as jnp
import numpy as np
from jax import lax

D = 256
BLOCK = 128
NB = 128
PAIRS = 64
LAYERS = 1
SPANS = 1024
NODES = 131072
RB = 16
CB = 64
K_MAX = 16
N_ROW = 64
N_COL = 16


def draw_block_ids(key, part):
    key = jax.random.fold_in(key, 11)
    grid_size = RB * CB
    scores = jax.random.randint(key, (SPANS, grid_size), 0, 1 << 16) * grid_size
    scores = scores + jnp.arange(grid_size, dtype=jnp.int32)[None, :]
    ranking = jnp.argsort(scores, axis=1, stable=True)
    return ranking[:, :K_MAX].astype(jnp.int32)


def draw_counts(key, part):
    key = jax.random.fold_in(key, 23)
    first_key, second_key = jax.random.split(key)
    lowest = max(1, K_MAX // 4)
    counts = jax.random.randint(first_key, (SPANS,), lowest, K_MAX + 1)
    fullest = jax.random.randint(second_key, (), 0, SPANS)
    return counts.at[fullest].set(K_MAX).astype(jnp.int32)


def plant(entries, key, least, largest):
    longest = entries.shape.index(max(entries.shape))
    spots = []
    for shift in (0, 1):
        where = [jax.random.randint(jax.random.fold_in(key, axis), (), 0, length) for axis, length in enumerate(entries.shape)]
        where[longest] = (where[longest] + shift) % entries.shape[longest]
        spots.append(tuple(where))
    return entries.at[spots[0]].set(least).at[spots[1]].set(largest)


def block_levels(own_key, extent, cuts, smallest, top_value):
    loudness = 1.0
    for dim, blocks in cuts:
        heights = jax.random.uniform(jax.random.fold_in(jax.random.fold_in(own_key, 6), dim), (blocks,), jnp.float32, smallest / len(cuts), top_value / len(cuts))
        loudness = loudness * jnp.repeat(jnp.exp(heights), extent[dim] // blocks).reshape((-1,) + (1,) * (len(extent) - 1 - dim))
    return loudness


def rank_table(count, lean):
    weights = [(1 << 20) // math.isqrt(standing ** lean) + 1 for standing in range(1, count + 1)]
    width = 1 + sum(weights) // (1 << 30)
    return np.cumsum(np.array([max(1, weight // width) for weight in weights]))


def ranked_ids(rng, extent, number_of, skew):
    listing = rank_table(number_of, skew)
    ticket = jax.random.randint(jax.random.fold_in(rng, 1), extent, 0, int(listing[number_of - 1]))
    grade = jnp.searchsorted(jnp.asarray(listing, jnp.int32), ticket, side="right")
    return jax.random.permutation(jax.random.fold_in(rng, 2), number_of)[grade].astype(jnp.int32)


def scatter_about(rng, shape, deviation, bound, pieces=(), held_as=jnp.bfloat16):
    result = jax.random.normal(rng, shape, jnp.float32) * deviation
    if len(pieces) > 0:
        result = block_levels(rng, shape, pieces, -0.22, 0.18) * result
    return jnp.clip(result, min=-bound, max=bound).astype(held_as)


def setup_inputs(seed: int = 0) -> dict:
    arg_keys = jax.random.split(jax.random.key(seed), 9)
    table = scatter_about(arg_keys[0], (NODES, D), 0.5, 3.0, ((0, 1024),), jnp.float32)
    blocks = jnp.clip(0.05 * jax.random.uniform(arg_keys[1], (SPANS, K_MAX, BLOCK, BLOCK), jnp.float32) ** block_levels(arg_keys[1], (SPANS, K_MAX, BLOCK, BLOCK), ((0, 1024),), -0.2, 0.2), 0.0, 0.05)
    block_ids = draw_block_ids(jax.random.fold_in(arg_keys[8], 71), 0)
    counts = draw_counts(jax.random.fold_in(arg_keys[8], 71), 0)
    users = plant(jax.random.randint(arg_keys[4], (SPANS, PAIRS), 0, NB), jax.random.fold_in(arg_keys[4], 1), 0, NB - 1).astype(jnp.int32)
    positives = plant(jax.random.randint(arg_keys[5], (SPANS, PAIRS), 0, NB), jax.random.fold_in(arg_keys[5], 1), 0, NB - 1).astype(jnp.int32)
    neg_index = plant(jax.random.randint(arg_keys[6], (SPANS, PAIRS), 0, PAIRS), jax.random.fold_in(arg_keys[6], 1), 0, PAIRS - 1).astype(jnp.int32)
    popular = plant(ranked_ids(arg_keys[7], (SPANS, PAIRS), NB, 2), jax.random.fold_in(arg_keys[7], 3), 0, NB - 1).astype(jnp.int32)
    return {"table": table, "blocks": blocks, "block_ids": block_ids, "counts": counts, "users": users, "positives": positives, "neg_index": neg_index, "popular": popular}


precise = lax.Precision.HIGHEST

def block_terms(source, values, positions, live_count, transpose):
    slot_count = values.shape[0]
    live_mask = (jnp.arange(slot_count, dtype=jnp.int32) < live_count).astype(values.dtype)
    row_hot = (positions[:, None] // CB == jnp.arange(RB, dtype=jnp.int32)[None, :]).astype(values.dtype)
    col_hot = (positions[:, None] % CB == jnp.arange(CB, dtype=jnp.int32)[None, :]).astype(values.dtype)
    if transpose:
        stacked = source.reshape(RB, BLOCK, D)
        picked = jnp.einsum('kr,rbd->kbd', row_hot * live_mask[:, None], stacked, precision=precise)
        products = jnp.einsum('kab,kad->kbd', values, picked, precision=precise)
        return jnp.einsum('kc,kbd->cbd', col_hot, products, precision=precise).reshape(CB * BLOCK, D)
    stacked = source.reshape(CB, BLOCK, D)
    picked = jnp.einsum('kc,cbd->kbd', col_hot * live_mask[:, None], stacked, precision=precise)
    products = jnp.einsum('kab,kbd->kad', values, picked, precision=precise)
    return jnp.einsum('kr,kad->rad', row_hot, products, precision=precise).reshape(RB * BLOCK, D)

def split_inputs(blocks, block_ids, counts):
    values = blocks.reshape(N_ROW, N_COL, K_MAX, BLOCK, BLOCK)
    positions = block_ids.reshape(N_ROW, N_COL, K_MAX)
    live_counts = counts.reshape(N_ROW, N_COL)
    return (values, positions, live_counts)

def spread(current, blocks, block_ids, counts):
    columns = current.reshape(N_ROW, N_COL, NB, D).transpose(1, 0, 2, 3).reshape(N_COL, N_ROW * NB, D)
    values, positions, live_counts = split_inputs(blocks, block_ids, counts)
    forward_terms = partial(block_terms, transpose=False)

    def one_row(inputs):
        values_row, positions_row, counts_row = inputs
        parts = jax.vmap(forward_terms)(columns, values_row, positions_row, counts_row)
        return lax.optimization_barrier(jnp.sum(parts, axis=0))
    return lax.map(one_row, (values, positions, live_counts)).reshape(NODES, D)

def spread_back(current, blocks, block_ids, counts):
    row_slabs = current.reshape(N_ROW, RB * BLOCK, D)
    values, positions, live_counts = split_inputs(blocks, block_ids, counts)
    back_terms = jax.vmap(partial(block_terms, transpose=True), in_axes=(None, 0, 0, 0))

    def one_row(carry, inputs):
        slab, values_row, positions_row, counts_row = inputs
        return (carry + back_terms(slab, values_row, positions_row, counts_row), None)
    start = jnp.zeros((N_COL, CB * BLOCK, D), current.dtype)
    summed, unused = lax.scan(one_row, start, (row_slabs, values, positions, live_counts))
    return summed.reshape(N_COL, N_ROW, NB, D).transpose(1, 0, 2, 3).reshape(NODES, D)

def pair_losses(table_rows, users, positives, neg_index, popular):
    user_rows = table_rows[users]
    item_rows = table_rows[positives]
    batch_rows = table_rows[positives[neg_index]]
    popular_rows = table_rows[popular]
    positive_score = lax.optimization_barrier(jnp.sum(user_rows * item_rows, axis=-1))
    first_terms = jax.nn.softplus(lax.optimization_barrier(jnp.sum(user_rows * batch_rows, axis=-1)) - positive_score)
    second_terms = jax.nn.softplus(lax.optimization_barrier(jnp.sum(user_rows * popular_rows, axis=-1)) - positive_score)
    return first_terms + second_terms

def reference(table, blocks, block_ids, counts, users, positives, neg_index, popular):
    current = table
    layer_sum = table
    for layer_index in range(LAYERS):
        current = spread(current, blocks, block_ids, counts)
        layer_sum = layer_sum + current
    final_rows = layer_sum / (LAYERS + 1)

    def all_losses(table_rows):
        return jax.vmap(pair_losses)(table_rows.reshape(SPANS, NB, D), users, positives, neg_index, popular)
    losses, pull = jax.vjp(all_losses, final_rows)
    final_grad = pull(jnp.ones_like(losses))[0]
    span_loss = lax.optimization_barrier(jnp.sum(losses, axis=1)) / PAIRS
    scaled = final_grad / (LAYERS + 1)
    gradient = scaled
    for layer_index in range(LAYERS):
        gradient = scaled + spread_back(gradient, blocks, block_ids, counts)
    return (gradient, span_loss)
```

```python
import functools

import jax
import jax.numpy as jnp
from jax import lax
from jax.experimental import pallas as pl
from jax.experimental.pallas import tpu as pltpu
from jax.sharding import PartitionSpec as P

BLOCK = 128
NX = 4
NZ = 16
NY = 8
HALF = 128
SLOTS = 16
RB = 16
CB = 64
HEAD = 8
VMEM_LIMIT = 48 * 1024 * 1024

precise = lax.Precision.HIGHEST

X_GROUPS = [[x * NZ + z for x in range(NX)] for z in range(NZ)]
Y_GROUPS = [[y * 2 + k for y in range(NY)] for k in range(2)]
CORE_GROUPS = [[2 * y, 2 * y + 1] for y in range(NY)]
Z_GROUPS = [[x * NZ + z for z in range(NZ)] for x in range(NX)]
Z_NEAR = [[x * NZ + 4 * a + b for b in range(4)] for x in range(NX) for a in range(4)]
Z_FAR = [[x * NZ + 4 * a + b for a in range(4)] for x in range(NX) for b in range(4)]
CORE_SWAP = [(i, i ^ 1) for i in range(2 * NY)]


def x_shift(step):
    return [(x * NZ + z, ((x + step) % NX) * NZ + z) for x in range(NX) for z in range(NZ)]


def exchange(values, axis, groups):
    return lax.all_to_all(
        values, axis, split_axis=0, concat_axis=0, tiled=True, axis_index_groups=groups
    )


def split_bf16(values):
    high = values.astype(jnp.bfloat16)
    low = (values - high.astype(jnp.float32)).astype(jnp.bfloat16)
    return high, low


def product(left, right_high, right_low, contract):
    left_high, left_low = split_bf16(left)
    dims = (((contract,), (0,)), ((), ()))

    def dot(a, b):
        return lax.dot_general(a, b, dims, preferred_element_type=jnp.float32)

    return dot(left_high, right_high) + (dot(left_high, right_low) + dot(left_low, right_high))


def block_kernel(transpose, place_ref, ids_ref, *refs):
    sources = refs[: 2 * NX]
    right_ref, out_ref, high_ref, low_ref = refs[2 * NX :]
    own_x = place_ref[0]
    out_ref[...] = jnp.zeros_like(out_ref)

    @pl.loop(0, right_ref.shape[0])
    def _(i):
        high, low = split_bf16(right_ref[i])
        high_ref[i] = high
        low_ref[i] = low

    for number, source in enumerate(sources):
        step, core = number // 2, number % 2
        row_x = lax.rem(own_x + (NX - step), NX)
        column_core = place_ref[1] if core == 0 else 1 - place_ref[1]

        @pl.loop(0, SLOTS)
        def _(slot):
            position = ids_ref[number * SLOTS + slot]
            column = lax.rem(jnp.maximum(position, 0), CB)
            live = jnp.logical_and(position >= 0, column // NZ == own_x)

            @pl.when(live)
            def _():
                row = row_x * RB + position // CB
                near = lax.rem(column, NZ) * 2 + column_core
                block = source[pl.ds(pl.multiple_of(slot * BLOCK, BLOCK), BLOCK), :]
                if transpose:
                    out_ref[near] += product(block, high_ref[row], low_ref[row], 0)
                else:
                    out_ref[row] += product(block, high_ref[near], low_ref[near], 1)


def multiply(place, ids, sources, right, transpose):
    rows = 2 * NZ if transpose else NX * RB
    return pl.pallas_call(
        functools.partial(block_kernel, transpose),
        out_shape=jax.ShapeDtypeStruct((rows, BLOCK, HALF), jnp.float32),
        in_specs=[pl.BlockSpec(memory_space=pltpu.SMEM)] * 2
        + [pl.BlockSpec(memory_space=pltpu.VMEM)] * (2 * NX + 1),
        out_specs=pl.BlockSpec(memory_space=pltpu.VMEM),
        scratch_shapes=[
            pltpu.VMEM(right.shape, jnp.bfloat16),
            pltpu.VMEM(right.shape, jnp.bfloat16),
        ],
        compiler_params=pltpu.CompilerParams(vmem_limit_bytes=VMEM_LIMIT),
    )(place, ids, *sources, right)


def swap_halves(rows):
    halves = rows.reshape(BLOCK, 2, HALF).transpose(1, 0, 2)
    return exchange(halves, "col", CORE_GROUPS)


def join_halves(pieces):
    halves = exchange(pieces, "col", CORE_GROUPS)
    return halves.transpose(1, 0, 2).reshape(BLOCK, 2 * HALF)


def one_hot(indices, span_rows):
    return (indices[:, None] == jnp.arange(span_rows, dtype=jnp.int32)[None, :]).astype(jnp.float32)


def per_device(table, blocks, block_ids, counts, users, positives, neg_index, popular):
    place = jnp.stack([lax.axis_index("row") // NZ, lax.axis_index("col") % 2]).astype(jnp.int32)

    halves = swap_halves(table)
    gathered = lax.all_gather(halves, "row", axis=0, tiled=True, axis_index_groups=Z_GROUPS)

    live = jnp.arange(SLOTS, dtype=jnp.int32) < counts[0]
    marked = jnp.where(live, block_ids[0], -1).astype(jnp.float32)
    header = jnp.pad(marked[None, :], ((0, HEAD - 1), (0, BLOCK - SLOTS)))
    packed = jnp.concatenate([blocks.reshape(SLOTS * BLOCK, BLOCK), header], axis=0)
    sources = []
    for step in range(NX):
        moved = packed if step == 0 else lax.ppermute(packed, "row", x_shift(step))
        sources += [moved, lax.ppermute(moved, "col", CORE_SWAP)]
    ids = jnp.concatenate([s[SLOTS * BLOCK, :SLOTS] for s in sources]).astype(jnp.int32)

    partial_rows = multiply(place, ids, sources, gathered, False)
    pieces = exchange(partial_rows.reshape(NX, RB * BLOCK, HALF), "row", X_GROUPS)
    summed = jnp.sum(pieces, axis=0).reshape(NY, 2 * BLOCK, HALF)
    pieces = exchange(summed, "col", Y_GROUPS)
    summed = jnp.sum(pieces, axis=0).reshape(2, BLOCK, HALF)
    current = join_halves(summed)

    final_rows = (table + current) / 2
    span_rows = table.shape[0]
    pick_user = one_hot(users[0], span_rows)
    pick_item = one_hot(positives[0], span_rows)
    pick_batch = one_hot(jnp.take(positives[0], neg_index[0]), span_rows)
    pick_popular = one_hot(popular[0], span_rows)

    def pair_losses(table_rows):
        user_rows = jnp.dot(pick_user, table_rows, precision=precise)
        item_rows = jnp.dot(pick_item, table_rows, precision=precise)
        batch_rows = jnp.dot(pick_batch, table_rows, precision=precise)
        popular_rows = jnp.dot(pick_popular, table_rows, precision=precise)
        positive_score = jnp.sum(user_rows * item_rows, axis=-1)
        first_terms = jax.nn.softplus(jnp.sum(user_rows * batch_rows, axis=-1) - positive_score)
        second_terms = jax.nn.softplus(jnp.sum(user_rows * popular_rows, axis=-1) - positive_score)
        return first_terms + second_terms

    losses, pull = jax.vjp(pair_losses, final_rows)
    final_grad = pull(jnp.ones_like(losses))[0]
    span_loss = (jnp.sum(losses) / losses.shape[0]).reshape(1)
    scaled = final_grad / 2

    halves = swap_halves(scaled).reshape(1, 2 * BLOCK, HALF)
    column = exchange(jnp.broadcast_to(halves, (NY, 2 * BLOCK, HALF)), "col", Y_GROUPS)
    column = column.reshape(1, RB * BLOCK, HALF)
    slab = exchange(jnp.broadcast_to(column, (NX, RB * BLOCK, HALF)), "row", X_GROUPS)
    partial_cols = multiply(place, ids, sources, slab.reshape(NX * RB, BLOCK, HALF), True)
    by_near = partial_cols.reshape(4, 4, 2 * BLOCK, HALF).transpose(1, 0, 2, 3)
    summed = jnp.sum(exchange(by_near, "row", Z_NEAR), axis=0)
    summed = jnp.sum(exchange(summed, "row", Z_FAR), axis=0)
    returned = join_halves(summed.reshape(2, BLOCK, HALF))
    return (scaled + returned, span_loss)


def solution(mesh):
    in_specs = (
        P(("row", "col"), None),
        P(("row", "col"), None, None, None),
        P(("row", "col"), None),
        P(("row", "col")),
        P(("row", "col"), None),
        P(("row", "col"), None),
        P(("row", "col"), None),
        P(("row", "col"), None),
    )
    out_specs = (P(("row", "col"), None), P(("row", "col")))
    return jax.shard_map(
        per_device, mesh=mesh, in_specs=in_specs, out_specs=out_specs, check_vma=False
    )
```

```python
import functools

import jax
import jax.numpy as jnp
from jax import lax
from jax.experimental import pallas as pl
from jax.experimental.pallas import tpu as pltpu
from jax.sharding import PartitionSpec as P

BLOCK = 128
NX = 4
NZ = 16
NY = 8
HALF = 128
SLOTS = 16
CB = 64
HEAD = 8
PAIRS = 64
VMEM_LIMIT = 48 * 1024 * 1024

precise = lax.Precision.HIGHEST

Y_GROUPS = [[y * 2 + k for y in range(NY)] for k in range(2)]
CORE_SWAP = [(i, i ^ 1) for i in range(2 * NY)]


def send_x(values, step):
    pairs = [(x * NZ + z, ((x + step) % NX) * NZ + z) for x in range(NX) for z in range(NZ)]
    return lax.ppermute(values, "row", pairs)


def send_z(values, step):
    pairs = [(x * NZ + z, x * NZ + (z + step) % NZ) for x in range(NX) for z in range(NZ)]
    return lax.ppermute(values, "row", pairs)


def swap_cores(values):
    return lax.ppermute(values, "col", CORE_SWAP)


def exchange_y(values):
    return lax.all_to_all(
        values, "col", split_axis=0, concat_axis=0, tiled=True, axis_index_groups=Y_GROUPS
    )


def split_bf16(values):
    high = values.astype(jnp.bfloat16)
    low = (values - high.astype(jnp.float32)).astype(jnp.bfloat16)
    return high, low


def product(left, right, contract):
    left_high, left_low = split_bf16(left)
    right_high, right_low = split_bf16(right)
    dims = (((contract,), (0,)), ((), ()))

    def dot(a, b):
        return lax.dot_general(a, b, dims, preferred_element_type=jnp.float32)

    return dot(left_high, right_high) + (dot(left_high, right_low) + dot(left_low, right_high))


def for_live_slots(place_ref, ids_ref, sources, body):
    own_x, own_z = place_ref[0], place_ref[1]
    for number, source in enumerate(sources):
        step, core = number // 2, number % 2

        @pl.loop(0, SLOTS)
        def _(slot):
            position = ids_ref[number * SLOTS + slot]
            column = jnp.bitwise_and(position, CB - 1)
            live = jnp.logical_and(position >= 0, column // NZ == own_x)

            @pl.when(live)
            def _():
                near = jnp.bitwise_and(column - own_z, NZ - 1) * 2 + core
                block = source[pl.ds(pl.multiple_of(slot * BLOCK, BLOCK), BLOCK), :]
                body(step, block, position // CB, near)


OWN = (0, 4, 8, 12)
AFTER = (1, 5, 9, 13)
BEFORE = (15, 3, 7, 11)
TWO_AFTER = (2, 6)
TWO_BEFORE = (14, 10)
PARTS = (OWN, AFTER, BEFORE, TWO_AFTER, TWO_BEFORE)


def forward_kernel(place_ref, ids_ref, *refs):
    sources, parts = refs[: 2 * NX], refs[2 * NX : 2 * NX + len(PARTS)]
    outs, rows_ref = refs[2 * NX + len(PARTS) : -1], refs[-1]
    for out in outs:
        out[...] = jnp.zeros_like(out)
    for part, distances in zip(parts, PARTS):
        for index, distance in enumerate(distances):
            rows_ref[pl.ds(2 * distance, 2)] = part[pl.ds(2 * index, 2)]

    def body(step, block, rb, near):
        value = product(block, rows_ref[near], 1)
        for half in range(2):

            @pl.when(rb % 2 == half)
            def _():
                outs[2 * step + half][rb // 2] += value

    for_live_slots(place_ref, ids_ref, sources, body)


def backward_kernel(place_ref, ids_ref, *refs):
    sources, slabs = refs[: 2 * NX], refs[2 * NX : 4 * NX]
    outs, total_ref = refs[4 * NX : -1], refs[-1]
    total_ref[...] = jnp.zeros_like(total_ref)

    def body(step, block, rb, near):
        first, second = slabs[2 * step], slabs[2 * step + 1]
        rows = jnp.where(rb % 2 == 0, first[rb // 2], second[rb // 2])
        total_ref[near] += product(block, rows, 0)

    for_live_slots(place_ref, ids_ref, sources, body)
    for out, distances in zip(outs, PARTS):
        for index, distance in enumerate(distances):
            out[pl.ds(2 * index, 2)] = total_ref[pl.ds(2 * distance, 2)]


def call_kernel(body, place, ids, arrays, out_blocks):
    whole = pl.BlockSpec(memory_space=pltpu.VMEM)
    return pl.pallas_call(
        body,
        out_shape=[jax.ShapeDtypeStruct((n, BLOCK, HALF), jnp.float32) for n in out_blocks],
        in_specs=[pl.BlockSpec(memory_space=pltpu.SMEM)] * 2 + [whole] * len(arrays),
        out_specs=[whole] * len(out_blocks),
        scratch_shapes=[pltpu.VMEM((2 * NZ, BLOCK, HALF), jnp.float32)],
        compiler_params=pltpu.CompilerParams(vmem_limit_bytes=VMEM_LIMIT),
    )(place, ids, *arrays)


def one_hot(indices, span_rows):
    return (indices[..., None] == jnp.arange(span_rows, dtype=jnp.int32)).astype(jnp.float32)


def per_device(table, blocks, block_ids, counts, users, positives, neg_index, popular):
    own_row = lax.axis_index("row")
    core = jnp.bitwise_and(lax.axis_index("col"), 1)
    place = jnp.stack([own_row // NZ, jnp.bitwise_and(own_row, NZ - 1)]).astype(jnp.int32)

    left, right = table[:, :HALF], table[:, HALF:]
    own_half = jnp.where(core == 0, left, right)
    other_half = swap_cores(jnp.where(core == 0, right, left))
    pair = jnp.stack([own_half, other_half])

    near_4 = jnp.concatenate([pair, send_z(pair, -4), send_z(pair, 8), send_z(pair, 4)])
    ends_after = near_4[:4]
    ends_before = jnp.concatenate([near_4[:2], near_4[6:]])

    live = jnp.arange(SLOTS, dtype=jnp.int32) < counts[0]
    marked = jnp.where(live, block_ids[0], -1).astype(jnp.float32)
    header = jnp.pad(marked[None, :], ((0, HEAD - 1), (0, BLOCK - SLOTS)))
    packed = jnp.concatenate([blocks.reshape(SLOTS * BLOCK, BLOCK), header], axis=0)
    sources = []
    for step in range(NX):
        moved = packed if step == 0 else send_x(packed, step)
        sources += [moved, swap_cores(moved)]
    ids = jnp.concatenate([s[SLOTS * BLOCK, :SLOTS] for s in sources]).astype(jnp.int32)

    parts = [
        near_4,
        send_z(near_4, -1),
        send_z(near_4, 1),
        send_z(ends_after, -2),
        send_z(ends_before, 2),
    ]
    partial_rows = call_kernel(forward_kernel, place, ids, sources + parts, [NY] * (2 * NX))
    current = []
    for half in range(2):
        summed = partial_rows[half]
        for step in range(1, NX):
            summed = summed + send_x(partial_rows[2 * step + half], -step)
        current.append(jnp.sum(exchange_y(summed), axis=0))

    picks = jnp.stack([users[0], positives[0], jnp.take(positives[0], neg_index[0]), popular[0]])
    other_picks = swap_cores(picks)
    is_first = core == 0
    span_picks = [jnp.where(is_first, picks, other_picks), jnp.where(is_first, other_picks, picks)]
    span_table = [
        jnp.where(is_first, own_half, other_half),
        jnp.where(is_first, other_half, own_half),
    ]
    final_rows = jnp.stack([(t + c) / 2 for t, c in zip(span_table, current)])
    hot = one_hot(jnp.stack(span_picks), BLOCK)
    rows = jnp.einsum("hpij,hjd->hpid", hot, final_rows, precision=precise)
    user_rows, item_rows, batch_rows, popular_rows = (rows[:, i] for i in range(4))
    scores = jnp.stack(
        [
            jnp.sum(user_rows * item_rows, axis=-1),
            jnp.sum(user_rows * batch_rows, axis=-1),
            jnp.sum(user_rows * popular_rows, axis=-1),
        ],
        axis=1,
    )
    scores = scores + swap_cores(scores)
    first = scores[:, 1] - scores[:, 0]
    second = scores[:, 2] - scores[:, 0]
    losses = jax.nn.softplus(first) + jax.nn.softplus(second)
    span_losses = jnp.sum(losses, axis=1) / PAIRS
    span_loss = jnp.where(is_first, span_losses[0], span_losses[1]).reshape(1)
    pull_first = jax.nn.sigmoid(first)[..., None] / 2
    pull_second = jax.nn.sigmoid(second)[..., None] / 2
    pull_item = -(pull_first + pull_second)
    row_grads = jnp.stack(
        [
            pull_item * item_rows + pull_first * batch_rows + pull_second * popular_rows,
            pull_item * user_rows,
            pull_first * user_rows,
            pull_second * user_rows,
        ],
        axis=1,
    )
    scaled = jnp.einsum("hpij,hpid->hjd", hot, row_grads, precision=precise)

    slabs = [None] * (2 * NX)
    for half in range(2):
        slab = exchange_y(jnp.broadcast_to(scaled[half][None], (NY, BLOCK, HALF)))
        slabs[half] = slab
        for step in range(1, NX):
            slabs[2 * step + half] = send_x(slab, step)
    own, after, before, two_after, two_before = call_kernel(
        backward_kernel, place, ids, sources + slabs, [2 * len(p) for p in PARTS]
    )
    after = send_z(after, 1)
    before = send_z(before, -1)
    two_after = send_z(two_after, 2)
    two_before = send_z(two_before, -2)
    sums = [own[2 * m : 2 * m + 2] + after[2 * m : 2 * m + 2] + before[2 * m : 2 * m + 2] for m in range(4)]
    sums[0] = sums[0] + two_after[:2] + two_before[:2]
    sums[1] = sums[1] + two_after[2:]
    sums[3] = sums[3] + two_before[2:]
    returned = sums[0] + send_z(sums[1], 4) + send_z(sums[3], -4) + send_z(sums[2], 8)

    scaled_own = jnp.where(is_first, scaled[0], scaled[1])
    scaled_other = jnp.where(is_first, scaled[1], scaled[0])
    own_grad = scaled_own + returned[0]
    other_grad = swap_cores(scaled_other + returned[1])
    gradient = jnp.where(
        is_first,
        jnp.concatenate([own_grad, other_grad], axis=1),
        jnp.concatenate([other_grad, own_grad], axis=1),
    )
    return (gradient, span_loss)


def solution(mesh):
    in_specs = (
        P(("row", "col"), None),
        P(("row", "col"), None, None, None),
        P(("row", "col"), None),
        P(("row", "col")),
        P(("row", "col"), None),
        P(("row", "col"), None),
        P(("row", "col"), None),
        P(("row", "col"), None),
    )
    out_specs = (P(("row", "col"), None), P(("row", "col")))
    return jax.shard_map(
        per_device, mesh=mesh, in_specs=in_specs, out_specs=out_specs, check_vma=False
    )
```

```python
import jax
import jax.numpy as jnp
from jax import lax
from jax.experimental import pallas as pl
from jax.experimental.pallas import tpu as pltpu
from jax.sharding import PartitionSpec as P

BLOCK = 128
NX = 4
NZ = 16
NY = 8
HALF = 128
SLOTS = 16
CB = 64
HEAD = 8
PAIRS = 64
VMEM_LIMIT = 48 * 1024 * 1024

precise = lax.Precision.HIGHEST

X_GROUPS = [[x * NZ + z for x in range(NX)] for z in range(NZ)]
Z_FAR = [[x * NZ + 4 * a + b for a in range(4)] for x in range(NX) for b in range(4)]
Y_GROUPS = [[y * 2 + k for y in range(NY)] for k in range(2)]
CORE_SWAP = [(i, i ^ 1) for i in range(2 * NY)]


def send_z(values, step):
    pairs = [(x * NZ + z, x * NZ + (z + step) % NZ) for x in range(NX) for z in range(NZ)]
    return lax.ppermute(values, "row", pairs)


def swap_cores(values):
    return lax.ppermute(values, "col", CORE_SWAP)


def exchange(values, axis, groups):
    return lax.all_to_all(
        values, axis, split_axis=0, concat_axis=0, tiled=True, axis_index_groups=groups
    )


def split_bf16(values):
    high = values.astype(jnp.bfloat16)
    low = (values - high.astype(jnp.float32)).astype(jnp.bfloat16)
    return high, low


def product(left, right, contract):
    left_high, left_low = split_bf16(left)
    right_high, right_low = split_bf16(right)
    dims = (((contract,), (0,)), ((), ()))

    def dot(a, b):
        return lax.dot_general(a, b, dims, preferred_element_type=jnp.float32)

    return dot(left_high, right_high) + (dot(left_high, right_low) + dot(left_low, right_high))


def for_live_slots(place_ref, ids_ref, sources, body):
    own_x, own_z = place_ref[0], place_ref[1]
    for core, source in enumerate(sources):

        @pl.loop(0, NX * SLOTS)
        def _(number):
            position = ids_ref[core * NX * SLOTS + number]
            column = jnp.bitwise_and(position, CB - 1)
            live = jnp.logical_and(position >= 0, column // NZ == own_x)

            @pl.when(live)
            def _():
                z = jnp.bitwise_and(column, NZ - 1)
                near = jnp.bitwise_and(z - own_z, 3) * 8 + (z // 4) * 2 + core
                step = number // SLOTS
                slot = jnp.bitwise_and(number, SLOTS - 1)
                start = step * (SLOTS * BLOCK + HEAD) + slot * BLOCK
                block = source[pl.ds(pl.multiple_of(start, 8), BLOCK), :]
                body(step, block, position // CB, near)


def forward_kernel(place_ref, ids_ref, source_ref, other_ref, own, after, two, two_far, before, *refs):
    by_span, rows_ref = refs[:2], refs[2]
    for out in by_span:
        out[...] = jnp.zeros_like(out)
    start = 0
    for part in (own, after, two, two_far, before):
        rows_ref[pl.ds(start, part.shape[0])] = part[...]
        start += part.shape[0]

    def body(step, block, rb, near):
        value = product(block, rows_ref[near], 1)

        @pl.when(rb % 2 == 0)
        def _():
            by_span[0][(rb // 2) * NX + step] += value

        @pl.when(rb % 2 == 1)
        def _():
            by_span[1][step * NY + rb // 2] += value

    for_live_slots(place_ref, ids_ref, (source_ref, other_ref), body)


def backward_kernel(place_ref, ids_ref, source_ref, other_ref, first, second, *refs):
    outs, total_ref = refs[:-1], refs[-1]
    total_ref[...] = jnp.zeros_like(total_ref)

    def body(step, block, rb, near):
        rows = jnp.where(
            rb % 2 == 0, first[(rb // 2) * NX + step], second[step * NY + rb // 2]
        )
        total_ref[near] += product(block, rows, 0)

    for_live_slots(place_ref, ids_ref, (source_ref, other_ref), body)
    start = 0
    for out in outs:
        out[...] = total_ref[pl.ds(start, out.shape[0])]
        start += out.shape[0]


def call_kernel(body, place, ids, arrays, out_blocks):
    whole = pl.BlockSpec(memory_space=pltpu.VMEM)
    return pl.pallas_call(
        body,
        out_shape=[jax.ShapeDtypeStruct((n, BLOCK, HALF), jnp.float32) for n in out_blocks],
        in_specs=[pl.BlockSpec(memory_space=pltpu.SMEM)] * 2 + [whole] * len(arrays),
        out_specs=[whole] * len(out_blocks),
        scratch_shapes=[pltpu.VMEM((2 * NZ, BLOCK, HALF), jnp.float32)],
        compiler_params=pltpu.CompilerParams(vmem_limit_bytes=VMEM_LIMIT),
    )(place, ids, *arrays)


def one_hot(indices, span_rows):
    return (indices[..., None] == jnp.arange(span_rows, dtype=jnp.int32)).astype(jnp.float32)


def per_device(table, blocks, block_ids, counts, users, positives, neg_index, popular):
    own_row = lax.axis_index("row")
    core = jnp.bitwise_and(lax.axis_index("col"), 1)
    place = jnp.stack([own_row // NZ, jnp.bitwise_and(own_row, NZ - 1)]).astype(jnp.int32)

    left, right = table[:, :HALF], table[:, HALF:]
    own_half = jnp.where(core == 0, left, right)
    other_half = swap_cores(jnp.where(core == 0, right, left))
    pair = jnp.stack([own_half, other_half])

    live = jnp.arange(SLOTS, dtype=jnp.int32) < counts[0]
    marked = jnp.where(live, block_ids[0], -1).astype(jnp.float32)
    header = jnp.pad(marked[None, :], ((0, HEAD - 1), (0, BLOCK - SLOTS)))
    packed = jnp.concatenate([blocks.reshape(SLOTS * BLOCK, BLOCK), header], axis=0)
    source = lax.all_gather(packed, "row", axis=0, tiled=True, axis_index_groups=X_GROUPS)
    other = swap_cores(source)
    ids = jnp.concatenate(
        [s.reshape(NX, -1, BLOCK)[:, SLOTS * BLOCK, :SLOTS].reshape(-1) for s in (source, other)]
    ).astype(jnp.int32)

    far = exchange(jnp.broadcast_to(pair[None], (4, 2, BLOCK, HALF)), "row", Z_FAR)
    far = far.reshape(8, BLOCK, HALF)
    parts = [far, send_z(far, -1), send_z(far[:4], -2), send_z(far[4:], 2), send_z(far, 1)]
    first, second = call_kernel(
        forward_kernel, place, ids, [source, other] + parts, [NX * NY] * 2
    )

    first = lax.psum_scatter(
        first.reshape(NY * NX, BLOCK, HALF),
        "col",
        scatter_dimension=0,
        tiled=True,
        axis_index_groups=Y_GROUPS,
    )
    second = jnp.sum(exchange(second.reshape(NX, NY, BLOCK, HALF), "row", X_GROUPS), axis=0)
    second = jnp.sum(exchange(second, "col", Y_GROUPS), axis=0)
    first = jnp.sum(exchange(first, "row", X_GROUPS), axis=0)
    current = [first, second]

    picks = jnp.stack([users[0], positives[0], jnp.take(positives[0], neg_index[0]), popular[0]])
    other_picks = swap_cores(picks)
    is_first = core == 0
    span_picks = [jnp.where(is_first, picks, other_picks), jnp.where(is_first, other_picks, picks)]
    span_table = [
        jnp.where(is_first, own_half, other_half),
        jnp.where(is_first, other_half, own_half),
    ]
    final_rows = jnp.stack([(t + c) / 2 for t, c in zip(span_table, current)])
    hot = one_hot(jnp.stack(span_picks), BLOCK)
    rows = jnp.einsum("hpij,hjd->hpid", hot, final_rows, precision=precise)
    user_rows, item_rows, batch_rows, popular_rows = (rows[:, i] for i in range(4))
    scores = jnp.stack(
        [
            jnp.sum(user_rows * item_rows, axis=-1),
            jnp.sum(user_rows * batch_rows, axis=-1),
            jnp.sum(user_rows * popular_rows, axis=-1),
        ],
        axis=1,
    )
    scores = scores + swap_cores(scores)
    first = scores[:, 1] - scores[:, 0]
    second = scores[:, 2] - scores[:, 0]
    losses = jax.nn.softplus(first) + jax.nn.softplus(second)
    span_losses = jnp.sum(losses, axis=1) / PAIRS
    span_loss = jnp.where(is_first, span_losses[0], span_losses[1]).reshape(1)
    pull_first = jax.nn.sigmoid(first)[..., None] / 2
    pull_second = jax.nn.sigmoid(second)[..., None] / 2
    pull_item = -(pull_first + pull_second)
    row_grads = jnp.stack(
        [
            pull_item * item_rows + pull_first * batch_rows + pull_second * popular_rows,
            pull_item * user_rows,
            pull_first * user_rows,
            pull_second * user_rows,
        ],
        axis=1,
    )
    scaled = jnp.einsum("hpij,hpid->hjd", hot, row_grads, precision=precise)

    first = exchange(jnp.broadcast_to(scaled[0][None], (NX, BLOCK, HALF)), "row", X_GROUPS)
    first = lax.all_gather(first, "col", axis=0, tiled=True, axis_index_groups=Y_GROUPS)
    second = exchange(jnp.broadcast_to(scaled[1][None], (NY, BLOCK, HALF)), "col", Y_GROUPS)
    second = jnp.broadcast_to(second[None], (NX, NY, BLOCK, HALF))
    second = exchange(second, "row", X_GROUPS).reshape(NX * NY, BLOCK, HALF)
    own, after, two, two_far, before = call_kernel(
        backward_kernel, place, ids, [source, other, first, second], [8, 8, 4, 4, 8]
    )
    two = jnp.concatenate([send_z(two, 2), send_z(two_far, -2)])
    near = own + send_z(after, 1) + send_z(before, -1) + two
    returned = jnp.sum(exchange(near.reshape(4, 2, BLOCK, HALF), "row", Z_FAR), axis=0)

    scaled_own = jnp.where(is_first, scaled[0], scaled[1])
    scaled_other = jnp.where(is_first, scaled[1], scaled[0])
    own_grad = scaled_own + returned[0]
    other_grad = swap_cores(scaled_other + returned[1])
    gradient = jnp.where(
        is_first,
        jnp.concatenate([own_grad, other_grad], axis=1),
        jnp.concatenate([other_grad, own_grad], axis=1),
    )
    return (gradient, span_loss)


def solution(mesh):
    in_specs = (
        P(("row", "col"), None),
        P(("row", "col"), None, None, None),
        P(("row", "col"), None),
        P(("row", "col")),
        P(("row", "col"), None),
        P(("row", "col"), None),
        P(("row", "col"), None),
        P(("row", "col"), None),
    )
    out_specs = (P(("row", "col"), None), P(("row", "col")))
    return jax.shard_map(
        per_device, mesh=mesh, in_specs=in_specs, out_specs=out_specs, check_vma=False
    )
```

```python
import jax
import jax.numpy as jnp
from jax import lax
from jax.experimental import pallas as pl
from jax.experimental.pallas import tpu as pltpu
from jax.sharding import PartitionSpec as P

BLOCK = 128
NX = 4
NZ = 16
NY = 8
HALF = 128
SLOTS = 16
CB = 64
HEAD = 8
PAIRS = 64
VMEM_LIMIT = 48 * 1024 * 1024

precise = lax.Precision.HIGHEST

X_GROUPS = [[x * NZ + z for x in range(NX)] for z in range(NZ)]
Z_FAR = [[x * NZ + 4 * a + b for a in range(4)] for x in range(NX) for b in range(4)]
Y_GROUPS = [[y * 2 + k for y in range(NY)] for k in range(2)]
CORE_SWAP = [(i, i ^ 1) for i in range(2 * NY)]


def send_z(values, step):
    pairs = [(x * NZ + z, x * NZ + (z + step) % NZ) for x in range(NX) for z in range(NZ)]
    return lax.ppermute(values, "row", pairs)


def swap_cores(values):
    return lax.ppermute(values, "col", CORE_SWAP)


def exchange(values, axis, groups):
    return lax.all_to_all(
        values, axis, split_axis=0, concat_axis=0, tiled=True, axis_index_groups=groups
    )


def split_bf16(values):
    high = values.astype(jnp.bfloat16)
    low = (values - high.astype(jnp.float32)).astype(jnp.bfloat16)
    return high, low


def product(left, right, contract):
    rows = jnp.concatenate(split_bf16(left), axis=1 - contract)
    columns = jnp.concatenate(split_bf16(right), axis=1)
    dims = (((contract,), (0,)), ((), ()))
    all_four = lax.dot_general(rows, columns, dims, preferred_element_type=jnp.float32)
    top, bottom = all_four[:BLOCK], all_four[BLOCK:]
    return top[:, :HALF] + (top[:, HALF:] + bottom[:, :HALF])


def for_live_slots(place_ref, ids_ref, sources, body):
    own_x, own_z = place_ref[0], place_ref[1]
    for core, source in enumerate(sources):

        @pl.loop(0, NX * SLOTS)
        def _(number):
            position = ids_ref[core * NX * SLOTS + number]
            column = jnp.bitwise_and(position, CB - 1)
            live = jnp.logical_and(position >= 0, column // NZ == own_x)

            @pl.when(live)
            def _():
                z = jnp.bitwise_and(column, NZ - 1)
                near = jnp.bitwise_and(z - own_z, 3) * 8 + (z // 4) * 2 + core
                step = number // SLOTS
                slot = jnp.bitwise_and(number, SLOTS - 1)
                start = step * (SLOTS * BLOCK + HEAD) + slot * BLOCK
                block = source[pl.ds(pl.multiple_of(start, 8), BLOCK), :]
                body(step, block, position // CB, near)


def forward_kernel(place_ref, ids_ref, source_ref, other_ref, own, after, two, two_far, before, *refs):
    by_span, rows_ref = refs[:2], refs[2]
    for out in by_span:
        out[...] = jnp.zeros_like(out)
    start = 0
    for part in (own, after, two, two_far, before):
        rows_ref[pl.ds(start, part.shape[0])] = part[...]
        start += part.shape[0]

    def body(step, block, rb, near):
        value = product(block, rows_ref[near], 1)

        @pl.when(rb % 2 == 0)
        def _():
            by_span[0][(rb // 2) * NX + step] += value

        @pl.when(rb % 2 == 1)
        def _():
            by_span[1][step * NY + rb // 2] += value

    for_live_slots(place_ref, ids_ref, (source_ref, other_ref), body)


def backward_kernel(place_ref, ids_ref, source_ref, other_ref, first, second, *refs):
    outs, total_ref = refs[:-1], refs[-1]
    total_ref[...] = jnp.zeros_like(total_ref)

    def body(step, block, rb, near):
        rows = jnp.where(
            rb % 2 == 0, first[(rb // 2) * NX + step], second[step * NY + rb // 2]
        )
        total_ref[near] += product(block, rows, 0)

    for_live_slots(place_ref, ids_ref, (source_ref, other_ref), body)
    start = 0
    for out in outs:
        out[...] = total_ref[pl.ds(start, out.shape[0])]
        start += out.shape[0]


def call_kernel(body, place, ids, arrays, out_blocks):
    whole = pl.BlockSpec(memory_space=pltpu.VMEM)
    return pl.pallas_call(
        body,
        out_shape=[jax.ShapeDtypeStruct((n, BLOCK, HALF), jnp.float32) for n in out_blocks],
        in_specs=[pl.BlockSpec(memory_space=pltpu.SMEM)] * 2 + [whole] * len(arrays),
        out_specs=[whole] * len(out_blocks),
        scratch_shapes=[pltpu.VMEM((2 * NZ, BLOCK, HALF), jnp.float32)],
        compiler_params=pltpu.CompilerParams(vmem_limit_bytes=VMEM_LIMIT),
    )(place, ids, *arrays)


def one_hot(indices, span_rows):
    return (indices[..., None] == jnp.arange(span_rows, dtype=jnp.int32)).astype(jnp.float32)


def per_device(table, blocks, block_ids, counts, users, positives, neg_index, popular):
    own_row = lax.axis_index("row")
    core = jnp.bitwise_and(lax.axis_index("col"), 1)
    place = jnp.stack([own_row // NZ, jnp.bitwise_and(own_row, NZ - 1)]).astype(jnp.int32)

    left, right = table[:, :HALF], table[:, HALF:]
    own_half = jnp.where(core == 0, left, right)
    other_half = swap_cores(jnp.where(core == 0, right, left))
    pair = jnp.stack([own_half, other_half])

    live = jnp.arange(SLOTS, dtype=jnp.int32) < counts[0]
    marked = jnp.where(live, block_ids[0], -1).astype(jnp.float32)
    header = jnp.pad(marked[None, :], ((0, HEAD - 1), (0, BLOCK - SLOTS)))
    packed = jnp.concatenate([blocks.reshape(SLOTS * BLOCK, BLOCK), header], axis=0)
    source = lax.all_gather(packed, "row", axis=0, tiled=True, axis_index_groups=X_GROUPS)

    far = exchange(jnp.broadcast_to(pair[None], (4, 2, BLOCK, HALF)), "row", Z_FAR)
    far = far.reshape(8, BLOCK, HALF)
    after, before = send_z(far, -1), send_z(far, 1)
    parts = [far, after, send_z(far[:4], -2), send_z(far[4:], 2), before]
    source, _, _ = lax.optimization_barrier((source, after, before))
    other = swap_cores(source)
    ids = jnp.concatenate(
        [s.reshape(NX, -1, BLOCK)[:, SLOTS * BLOCK, :SLOTS].reshape(-1) for s in (source, other)]
    ).astype(jnp.int32)
    first, second = call_kernel(
        forward_kernel, place, ids, [source, other] + parts, [NX * NY] * 2
    )

    first = lax.psum_scatter(
        first.reshape(NY * NX, BLOCK, HALF),
        "col",
        scatter_dimension=0,
        tiled=True,
        axis_index_groups=Y_GROUPS,
    )
    second = jnp.sum(exchange(second.reshape(NX, NY, BLOCK, HALF), "row", X_GROUPS), axis=0)
    second = jnp.sum(exchange(second, "col", Y_GROUPS), axis=0)
    first = jnp.sum(exchange(first, "row", X_GROUPS), axis=0)
    current = [first, second]

    picks = jnp.stack([users[0], positives[0], jnp.take(positives[0], neg_index[0]), popular[0]])
    other_picks = swap_cores(picks)
    is_first = core == 0
    span_picks = [jnp.where(is_first, picks, other_picks), jnp.where(is_first, other_picks, picks)]
    span_table = [
        jnp.where(is_first, own_half, other_half),
        jnp.where(is_first, other_half, own_half),
    ]
    final_rows = jnp.stack([(t + c) / 2 for t, c in zip(span_table, current)])
    hot = one_hot(jnp.stack(span_picks), BLOCK)
    rows = jnp.einsum("hpij,hjd->hpid", hot, final_rows, precision=precise)
    user_rows, item_rows, batch_rows, popular_rows = (rows[:, i] for i in range(4))
    scores = jnp.stack(
        [
            jnp.sum(user_rows * item_rows, axis=-1),
            jnp.sum(user_rows * batch_rows, axis=-1),
            jnp.sum(user_rows * popular_rows, axis=-1),
        ],
        axis=1,
    )
    scores = scores + swap_cores(scores)
    first = scores[:, 1] - scores[:, 0]
    second = scores[:, 2] - scores[:, 0]
    losses = jax.nn.softplus(first) + jax.nn.softplus(second)
    span_losses = jnp.sum(losses, axis=1) / PAIRS
    span_loss = jnp.where(is_first, span_losses[0], span_losses[1]).reshape(1)
    pull_first = jax.nn.sigmoid(first)[..., None] / 2
    pull_second = jax.nn.sigmoid(second)[..., None] / 2
    pull_item = -(pull_first + pull_second)
    row_grads = jnp.stack(
        [
            pull_item * item_rows + pull_first * batch_rows + pull_second * popular_rows,
            pull_item * user_rows,
            pull_first * user_rows,
            pull_second * user_rows,
        ],
        axis=1,
    )
    scaled = jnp.einsum("hpij,hpid->hjd", hot, row_grads, precision=precise)

    first = exchange(jnp.broadcast_to(scaled[0][None], (NX, BLOCK, HALF)), "row", X_GROUPS)
    first = lax.all_gather(first, "col", axis=0, tiled=True, axis_index_groups=Y_GROUPS)
    second = exchange(jnp.broadcast_to(scaled[1][None], (NY, BLOCK, HALF)), "col", Y_GROUPS)
    second = jnp.broadcast_to(second[None], (NX, NY, BLOCK, HALF))
    second = exchange(second, "row", X_GROUPS).reshape(NX * NY, BLOCK, HALF)
    own, after, two, two_far, before = call_kernel(
        backward_kernel, place, ids, [source, other, first, second], [8, 8, 4, 4, 8]
    )
    two = jnp.concatenate([send_z(two, 2), send_z(two_far, -2)])
    near = own + send_z(after, 1) + send_z(before, -1) + two
    returned = jnp.sum(exchange(near.reshape(4, 2, BLOCK, HALF), "row", Z_FAR), axis=0)

    scaled_own = jnp.where(is_first, scaled[0], scaled[1])
    scaled_other = jnp.where(is_first, scaled[1], scaled[0])
    own_grad = scaled_own + returned[0]
    other_grad = swap_cores(scaled_other + returned[1])
    gradient = jnp.where(
        is_first,
        jnp.concatenate([own_grad, other_grad], axis=1),
        jnp.concatenate([other_grad, own_grad], axis=1),
    )
    return (gradient, span_loss)


def solution(mesh):
    in_specs = (
        P(("row", "col"), None),
        P(("row", "col"), None, None, None),
        P(("row", "col"), None),
        P(("row", "col")),
        P(("row", "col"), None),
        P(("row", "col"), None),
        P(("row", "col"), None),
        P(("row", "col"), None),
    )
    out_specs = (P(("row", "col"), None), P(("row", "col")))
    return jax.shard_map(
        per_device, mesh=mesh, in_specs=in_specs, out_specs=out_specs, check_vma=False
    )
```

```python
import jax
import jax.numpy as jnp
from jax import lax
from jax.experimental import pallas as pl
from jax.experimental.pallas import tpu as pltpu
from jax.sharding import PartitionSpec as P

BLOCK = 128
NX = 4
NZ = 16
NY = 8
HALF = 128
SLOTS = 16
CB = 64
HEAD = 8
PAIRS = 64
STRIDE = SLOTS * BLOCK + HEAD
EXTRA = 32
VMEM_LIMIT = 48 * 1024 * 1024

precise = lax.Precision.HIGHEST

BOTH = ("row", "col")
X_GROUPS = [[x * NZ + z for x in range(NX)] for z in range(NZ)]
Y_GROUPS = [[y * 2 + k for y in range(NY)] for k in range(2)]
X_CORE = [
    [(x * NZ + z) * 2 * NY + 2 * y + k for x in range(NX) for k in range(2)]
    for z in range(NZ)
    for y in range(NY)
]
Z_CORE = [
    [(x * NZ + 4 * a + b) * 2 * NY + 2 * y + k for a in range(4) for k in range(2)]
    for x in range(NX)
    for b in range(4)
    for y in range(NY)
]
CORE_SWAP = [(i, i ^ 1) for i in range(2 * NY)]


def send_z(values, step):
    pairs = [(x * NZ + z, x * NZ + (z + step) % NZ) for x in range(NX) for z in range(NZ)]
    return lax.ppermute(values, "row", pairs)


def swap_cores(values):
    return lax.ppermute(values, "col", CORE_SWAP)


def exchange(values, axis, groups):
    return lax.all_to_all(
        values, axis, split_axis=0, concat_axis=0, tiled=True, axis_index_groups=groups
    )


def split_bf16(values):
    high = values.astype(jnp.bfloat16)
    low = (values - high.astype(jnp.float32)).astype(jnp.bfloat16)
    return high, low


def product(left, right, contract):
    rows = jnp.concatenate(split_bf16(left), axis=1 - contract)
    columns = jnp.concatenate(split_bf16(right), axis=1)
    dims = (((contract,), (0,)), ((), ()))
    all_four = lax.dot_general(rows, columns, dims, preferred_element_type=jnp.float32)
    top, bottom = all_four[:BLOCK], all_four[BLOCK:]
    return top[:, :HALF] + (top[:, HALF:] + bottom[:, :HALF])


def start_copies(place_ref, ids_ref, source_ref, blocks_ref, order_ref, arrived):
    def visit(number, count):
        position = ids_ref[number]
        column = jnp.bitwise_and(position, CB - 1)
        live = jnp.logical_and(position >= 0, column // NZ == place_ref[0])

        @pl.when(live)
        def _():
            order_ref[count] = number
            copy_block(number, count, source_ref, blocks_ref, arrived).start()

        return count + live.astype(jnp.int32)

    return lax.fori_loop(0, 2 * NX * SLOTS, visit, jnp.int32(0))


def copy_block(number, place, source_ref, blocks_ref, arrived):
    start = (number // SLOTS) * STRIDE + jnp.bitwise_and(number, SLOTS - 1) * BLOCK
    rows = source_ref.at[pl.ds(pl.multiple_of(start, 8), BLOCK)]
    return pltpu.make_async_copy(rows, blocks_ref.at[place], arrived.at[place])


def for_live_blocks(count, place_ref, ids_ref, source_ref, blocks_ref, order_ref, arrived, body):
    @pl.loop(0, count)
    def _(index):
        number = order_ref[index]
        position = ids_ref[number]
        z = jnp.bitwise_and(position, NZ - 1)
        near = jnp.bitwise_and(z - place_ref[1], 3) * 8 + (z // 4) * 2
        near = near + jnp.bitwise_and(number // SLOTS, 1)
        copy_block(number, index, source_ref, blocks_ref, arrived).wait()
        body(number // (2 * SLOTS), blocks_ref[index], position // CB, near)


def forward_kernel(place_ref, ids_ref, source_ref, *refs):
    parts, (first, second), rows_ref, rest = refs[:5], refs[5:7], refs[7], refs[8:]
    count = start_copies(place_ref, ids_ref, source_ref, *rest)
    first[...] = jnp.zeros_like(first)
    second[...] = jnp.zeros_like(second)
    start = 0
    for part in parts:
        rows_ref[pl.ds(start, part.shape[0])] = part[...]
        start += part.shape[0]

    def body(x, block, rb, near):
        value = product(block, rows_ref[near], 1)
        y = rb // 2

        @pl.when(rb % 2 == 0)
        def _():
            first[y * NX + x, pl.ds(0, BLOCK)] += value

        @pl.when(rb % 2 == 1)
        def _():
            first[y * NX + x, pl.ds(BLOCK, EXTRA)] += value[:EXTRA]
            second[x * NY + y] += value[EXTRA:]

    for_live_blocks(count, place_ref, ids_ref, source_ref, *rest, body)


def backward_kernel(place_ref, ids_ref, source_ref, first, second, *refs):
    outs, total_ref, rest = refs[:5], refs[5], refs[6:]
    count = start_copies(place_ref, ids_ref, source_ref, *rest)
    total_ref[...] = jnp.zeros_like(total_ref)

    def body(x, block, rb, near):
        y = rb // 2
        rows = jnp.where(rb % 2 == 0, first[y * NX + x], second[x * NY + y])
        total_ref[near] += product(block, rows, 0)

    for_live_blocks(count, place_ref, ids_ref, source_ref, *rest, body)
    start = 0
    for out in outs:
        out[...] = total_ref[pl.ds(start, out.shape[0])]
        start += out.shape[0]


def call_kernel(body, place, ids, source, arrays, out_shapes):
    whole = pl.BlockSpec(memory_space=pltpu.VMEM)
    scalars = pl.BlockSpec(memory_space=pltpu.SMEM)
    slots = 2 * NX * SLOTS
    return pl.pallas_call(
        body,
        out_shape=[jax.ShapeDtypeStruct((*shape, HALF), jnp.float32) for shape in out_shapes],
        in_specs=[scalars, scalars, pl.BlockSpec(memory_space=pl.ANY)] + [whole] * len(arrays),
        out_specs=[whole] * len(out_shapes),
        scratch_shapes=[
            pltpu.VMEM((2 * NZ, BLOCK, HALF), jnp.float32),
            pltpu.VMEM((slots, BLOCK, BLOCK), jnp.float32),
            pltpu.SMEM((slots,), jnp.int32),
            pltpu.SemaphoreType.DMA((slots,)),
        ],
        compiler_params=pltpu.CompilerParams(vmem_limit_bytes=VMEM_LIMIT),
    )(place, ids, source, *arrays)


def one_hot(indices, span_rows):
    return (indices[..., None] == jnp.arange(span_rows, dtype=jnp.int32)).astype(jnp.float32)


def per_device(table, blocks, block_ids, counts, users, positives, neg_index, popular):
    own_row = lax.axis_index("row")
    core = jnp.bitwise_and(lax.axis_index("col"), 1)
    own_z = jnp.bitwise_and(own_row, NZ - 1)
    place = jnp.stack([own_row // NZ, own_z]).astype(jnp.int32)

    live = jnp.arange(SLOTS, dtype=jnp.int32) < counts[0]
    marked = jnp.where(live, block_ids[0], -1).astype(jnp.float32)
    header = jnp.pad(marked[None, :], ((0, HEAD - 1), (0, BLOCK - SLOTS)))
    packed = jnp.concatenate([blocks.reshape(SLOTS * BLOCK, BLOCK), header], axis=0)
    source = lax.all_gather(packed, BOTH, axis=0, tiled=True, axis_index_groups=X_CORE)

    halves = jnp.stack([table[:, :HALF], table[:, HALF:]])
    halves = jnp.broadcast_to(halves[None], (4, 2, BLOCK, HALF)).reshape(8, BLOCK, HALF)
    far = exchange(halves, BOTH, Z_CORE)
    span_table = lax.dynamic_slice_in_dim(far, own_z // 4 * 2, 2)
    parts = [far, send_z(far, -1), send_z(far[:4], -2), send_z(far[4:], 2), send_z(far, 1)]
    picks = jnp.stack([users[0], positives[0], jnp.take(positives[0], neg_index[0]), popular[0]])
    other_picks = swap_cores(picks)
    source, other_picks, *parts = lax.optimization_barrier((source, other_picks, *parts))
    ids = source.reshape(2 * NX, STRIDE, BLOCK)[:, SLOTS * BLOCK, :SLOTS].reshape(-1).astype(jnp.int32)
    shapes = [(NX * NY, BLOCK + EXTRA), (NX * NY, BLOCK - EXTRA)]
    first, second = call_kernel(forward_kernel, place, ids, source, parts, shapes)

    first = lax.psum_scatter(
        first, "col", scatter_dimension=0, tiled=True, axis_index_groups=Y_GROUPS
    )
    second = second.reshape(NX, NY, BLOCK - EXTRA, HALF)
    second = jnp.sum(exchange(second, "row", X_GROUPS), axis=0)
    second = jnp.sum(exchange(second, "col", Y_GROUPS), axis=0)
    first = jnp.sum(exchange(first, "row", X_GROUPS), axis=0)
    current = jnp.concatenate([first, second]).reshape(2, BLOCK, HALF)

    is_first = core == 0
    span_picks = [jnp.where(is_first, picks, other_picks), jnp.where(is_first, other_picks, picks)]
    final_rows = (span_table + current) / 2
    hot = one_hot(jnp.stack(span_picks), BLOCK)
    rows = jnp.einsum("hpij,hjd->hpid", hot, final_rows, precision=precise)
    user_rows, item_rows, batch_rows, popular_rows = (rows[:, i] for i in range(4))
    scores = jnp.stack(
        [
            jnp.sum(user_rows * item_rows, axis=-1),
            jnp.sum(user_rows * batch_rows, axis=-1),
            jnp.sum(user_rows * popular_rows, axis=-1),
        ],
        axis=1,
    )
    scores = scores + swap_cores(scores)
    first = scores[:, 1] - scores[:, 0]
    second = scores[:, 2] - scores[:, 0]
    losses = jax.nn.softplus(first) + jax.nn.softplus(second)
    span_losses = jnp.sum(losses, axis=1) / PAIRS
    span_loss = jnp.where(is_first, span_losses[0], span_losses[1]).reshape(1)
    pull_first = jax.nn.sigmoid(first)[..., None] / 2
    pull_second = jax.nn.sigmoid(second)[..., None] / 2
    pull_item = -(pull_first + pull_second)
    row_grads = jnp.stack(
        [
            pull_item * item_rows + pull_first * batch_rows + pull_second * popular_rows,
            pull_item * user_rows,
            pull_first * user_rows,
            pull_second * user_rows,
        ],
        axis=1,
    )
    scaled = jnp.einsum("hpij,hpid->hjd", hot, row_grads, precision=precise)

    first = exchange(jnp.broadcast_to(scaled[0][None], (NX, BLOCK, HALF)), "row", X_GROUPS)
    first = lax.all_gather(first, "col", axis=0, tiled=True, axis_index_groups=Y_GROUPS)
    second = exchange(jnp.broadcast_to(scaled[1][None], (NY, BLOCK, HALF)), "col", Y_GROUPS)
    second = jnp.broadcast_to(second[None], (NX, NY, BLOCK, HALF))
    second = exchange(second, "row", X_GROUPS).reshape(NX * NY, BLOCK, HALF)
    shapes = [(n, BLOCK) for n in (8, 8, 4, 4, 8)]
    own, after, two, two_far, before = call_kernel(
        backward_kernel, place, ids, source, [first, second], shapes
    )
    two = jnp.concatenate([send_z(two, 2), send_z(two_far, -2)])
    near = (own + send_z(after, 1) + send_z(before, -1) + two).reshape(4, 2, BLOCK, HALF)
    is_own = (jnp.arange(4) == own_z // 4)[:, None, None, None]
    near = near + jnp.where(is_own, scaled[None], 0.0)
    halves = exchange(near.reshape(8, BLOCK, HALF), BOTH, Z_CORE)
    halves = jnp.sum(halves.reshape(4, 2, BLOCK, HALF), axis=0)
    gradient = jnp.concatenate([halves[0], halves[1]], axis=1)
    return (gradient, span_loss)


def solution(mesh):
    in_specs = (
        P(("row", "col"), None),
        P(("row", "col"), None, None, None),
        P(("row", "col"), None),
        P(("row", "col")),
        P(("row", "col"), None),
        P(("row", "col"), None),
        P(("row", "col"), None),
        P(("row", "col"), None),
    )
    out_specs = (P(("row", "col"), None), P(("row", "col")))
    return jax.shard_map(
        per_device, mesh=mesh, in_specs=in_specs, out_specs=out_specs, check_vma=False
    )
```

```python
import functools

import jax
import jax.numpy as jnp
from jax import lax
from jax.experimental import pallas as pl
from jax.experimental.pallas import tpu as pltpu
from jax.sharding import PartitionSpec as P

BLOCK = 128
NX = 4
NZ = 16
NY = 8
HALF = 128
SLOTS = 16
CB = 64
PAIRS = 64
ENTRIES = 2 * NX * SLOTS
VMEM_LIMIT = 48 * 1024 * 1024

precise = lax.Precision.HIGHEST

BOTH = ("row", "col")
X_GROUPS = [[x * NZ + z for x in range(NX)] for z in range(NZ)]
Y_GROUPS = [[y * 2 + k for y in range(NY)] for k in range(2)]
X_CORE = [
    [(x * NZ + z) * 2 * NY + 2 * y + k for x in range(NX) for k in range(2)]
    for z in range(NZ)
    for y in range(NY)
]
Z_CORE = [
    [(x * NZ + 4 * a + b) * 2 * NY + 2 * y + k for a in range(4) for k in range(2)]
    for x in range(NX)
    for b in range(4)
    for y in range(NY)
]
CORE_SWAP = [(i, i ^ 1) for i in range(2 * NY)]


def send_z(values, step):
    pairs = [(x * NZ + z, x * NZ + (z + step) % NZ) for x in range(NX) for z in range(NZ)]
    return lax.ppermute(values, "row", pairs)


def swap_cores(values):
    return lax.ppermute(values, "col", CORE_SWAP)


def exchange(values, axis, groups):
    return lax.all_to_all(
        values, axis, split_axis=0, concat_axis=0, tiled=True, axis_index_groups=groups
    )


def split_bf16(values):
    high = values.astype(jnp.bfloat16)
    low = (values - high.astype(jnp.float32)).astype(jnp.bfloat16)
    return high, low


def product(left, right, contract):
    left_high, left_low = split_bf16(left)
    right_high, right_low = split_bf16(right)
    rows = jnp.concatenate([left_high, left_low, left_high], axis=contract)
    columns = jnp.concatenate([right_high, right_high, right_low], axis=0)
    dims = (((contract,), (0,)), ((), ()))
    return lax.dot_general(rows, columns, dims, preferred_element_type=jnp.float32)


def copy_block(entry, place, source_ref, blocks_ref, arrived):
    rows = source_ref.at[jnp.bitwise_and(entry, ENTRIES - 1)]
    return pltpu.make_async_copy(rows, blocks_ref.at[place], arrived.at[place])


def start_copies(first, last, list_ref, source_ref, blocks_ref, arrived):
    @pl.loop(first, last)
    def _(index):
        copy_block(list_ref[index], index, source_ref, blocks_ref, arrived).start()


def for_live_blocks(first, last, place_ref, list_ref, source_ref, blocks_ref, arrived, body):
    @pl.loop(first, last)
    def _(index):
        entry = list_ref[index]
        number, position = jnp.bitwise_and(entry, ENTRIES - 1), entry // ENTRIES
        z = jnp.bitwise_and(position, NZ - 1)
        near = jnp.bitwise_and(z - place_ref[0], 3) * 8 + (z // 4) * 2
        near = near + jnp.bitwise_and(number // SLOTS, 1)
        copy_block(entry, index, source_ref, blocks_ref, arrived).wait()
        body(number // (2 * SLOTS), blocks_ref[index], position // (2 * CB), near, index)


def forward_kernel(odd, place_ref, list_ref, source_ref, *refs):
    parts, out_ref, rows_ref, rest = refs[:5], refs[5], refs[6], refs[7:]
    first = place_ref[1] if odd else 0
    last = place_ref[2] if odd else place_ref[1]
    start_copies(first, last, list_ref, source_ref, *rest)
    out_ref[...] = jnp.zeros_like(out_ref)
    start = 0
    for part in parts:
        rows_ref[pl.ds(start, part.shape[0])] = part[...]
        start += part.shape[0]

    def body(x, block, y, near, index):
        place = x * NY + y if odd else y * NX + x
        out_ref[place] += product(block, rows_ref[near], 1)

    for_live_blocks(first, last, place_ref, list_ref, source_ref, *rest, body)


def backward_kernel(place_ref, list_ref, source_ref, even, odd, *refs):
    outs, total_ref, rest = refs[:5], refs[5], refs[6:]
    start_copies(0, place_ref[2], list_ref, source_ref, *rest)
    total_ref[...] = jnp.zeros_like(total_ref)

    def body(x, block, y, near, index):
        rows = jnp.where(index < place_ref[1], even[y * NX + x], odd[x * NY + y])
        total_ref[near] += product(block, rows, 0)

    for_live_blocks(0, place_ref[2], place_ref, list_ref, source_ref, *rest, body)
    start = 0
    for out in outs:
        out[...] = total_ref[pl.ds(start, out.shape[0])]
        start += out.shape[0]


def call_kernel(body, place, entries, source, arrays, out_blocks):
    whole = pl.BlockSpec(memory_space=pltpu.VMEM)
    scalars = pl.BlockSpec(memory_space=pltpu.SMEM)
    return pl.pallas_call(
        body,
        out_shape=[jax.ShapeDtypeStruct((n, BLOCK, HALF), jnp.float32) for n in out_blocks],
        in_specs=[scalars, scalars, pl.BlockSpec(memory_space=pl.ANY)] + [whole] * len(arrays),
        out_specs=[whole] * len(out_blocks),
        scratch_shapes=[
            pltpu.VMEM((2 * NZ, BLOCK, HALF), jnp.float32),
            pltpu.VMEM((ENTRIES, BLOCK, BLOCK), jnp.float32),
            pltpu.SemaphoreType.DMA((ENTRIES,)),
        ],
        compiler_params=pltpu.CompilerParams(vmem_limit_bytes=VMEM_LIMIT),
    )(place, entries, source, *arrays)


def live_list(ids, own_x, own_z):
    numbers = jnp.arange(ENTRIES, dtype=jnp.int32)
    live = (ids >= 0) & (jnp.bitwise_and(ids, CB - 1) // NZ == own_x)
    odd = jnp.bitwise_and(ids // CB, 1) == 1
    even_live, odd_live = live & ~odd, live & odd
    before = numbers[None, :] < numbers[:, None]
    even_end = jnp.sum(even_live.astype(jnp.int32))
    rank = jnp.where(
        odd,
        even_end + jnp.sum((before & odd_live[None, :]).astype(jnp.int32), axis=1),
        jnp.sum((before & even_live[None, :]).astype(jnp.int32), axis=1),
    )
    hit = live[None, :] & (rank[None, :] == numbers[:, None])
    entries = jnp.sum(jnp.where(hit, (ids * ENTRIES + numbers)[None, :], 0), axis=1)
    return entries, jnp.stack([own_z, even_end, jnp.sum(live.astype(jnp.int32))])


def one_hot(indices, span_rows):
    return (indices[..., None] == jnp.arange(span_rows, dtype=jnp.int32)).astype(jnp.float32)


def per_device(table, blocks, block_ids, counts, users, positives, neg_index, popular):
    own_row = lax.axis_index("row")
    core = jnp.bitwise_and(lax.axis_index("col"), 1)
    own_z = jnp.bitwise_and(own_row, NZ - 1)
    source = lax.all_gather(blocks[0], BOTH, axis=0, tiled=True, axis_index_groups=X_CORE)

    halves = jnp.stack([table[:, :HALF], table[:, HALF:]])
    halves = jnp.broadcast_to(halves[None], (4, 2, BLOCK, HALF)).reshape(8, BLOCK, HALF)
    far = exchange(halves, BOTH, Z_CORE)
    span_table = lax.dynamic_slice_in_dim(far, own_z // 4 * 2, 2)
    parts = [far, send_z(far, -1), send_z(far[:4], -2), send_z(far[4:], 2), send_z(far, 1)]
    picks = jnp.stack([users[0], positives[0], jnp.take(positives[0], neg_index[0]), popular[0]])
    other_picks = swap_cores(picks)
    live = jnp.arange(SLOTS, dtype=jnp.int32) < counts[0]
    marked, _ = lax.optimization_barrier((jnp.where(live, block_ids[0], -1), far))
    ids = exchange(jnp.broadcast_to(marked[None], (2 * NX, SLOTS)), BOTH, X_CORE)
    entries, place = live_list(ids.reshape(-1), own_row // NZ, own_z)
    source, other_picks, entries, place, *parts = lax.optimization_barrier(
        (source, other_picks, entries, place, *parts)
    )
    even, odd = (functools.partial(forward_kernel, odd) for odd in (False, True))
    (first,) = call_kernel(even, place, entries, source, parts, [NX * NY])
    entries, first = lax.optimization_barrier((entries, first))
    (second,) = call_kernel(odd, place, entries, source, parts, [NX * NY])

    first = lax.psum_scatter(
        first, "col", scatter_dimension=0, tiled=True, axis_index_groups=Y_GROUPS
    )
    second = second.reshape(NX, NY, BLOCK, HALF)
    second = jnp.sum(exchange(second, "row", X_GROUPS), axis=0)
    second = jnp.sum(exchange(second, "col", Y_GROUPS), axis=0)
    first = jnp.sum(exchange(first, "row", X_GROUPS), axis=0)
    current = jnp.stack([first, second])

    is_first = core == 0
    span_picks = [jnp.where(is_first, picks, other_picks), jnp.where(is_first, other_picks, picks)]
    final_rows = (span_table + current) / 2
    hot = one_hot(jnp.stack(span_picks), BLOCK)
    rows = jnp.einsum("hpij,hjd->hpid", hot, final_rows, precision=precise)
    user_rows, item_rows, batch_rows, popular_rows = (rows[:, i] for i in range(4))
    scores = jnp.stack(
        [
            jnp.sum(user_rows * item_rows, axis=-1),
            jnp.sum(user_rows * batch_rows, axis=-1),
            jnp.sum(user_rows * popular_rows, axis=-1),
        ],
        axis=1,
    )
    scores = scores + swap_cores(scores)
    first = scores[:, 1] - scores[:, 0]
    second = scores[:, 2] - scores[:, 0]
    losses = jax.nn.softplus(first) + jax.nn.softplus(second)
    span_losses = jnp.sum(losses, axis=1) / PAIRS
    span_loss = jnp.where(is_first, span_losses[0], span_losses[1]).reshape(1)
    pull_first = jax.nn.sigmoid(first)[..., None] / 2
    pull_second = jax.nn.sigmoid(second)[..., None] / 2
    pull_item = -(pull_first + pull_second)
    row_grads = jnp.stack(
        [
            pull_item * item_rows + pull_first * batch_rows + pull_second * popular_rows,
            pull_item * user_rows,
            pull_first * user_rows,
            pull_second * user_rows,
        ],
        axis=1,
    )
    scaled = jnp.einsum("hpij,hpid->hjd", hot, row_grads, precision=precise)

    first = exchange(jnp.broadcast_to(scaled[0][None], (NX, BLOCK, HALF)), "row", X_GROUPS)
    first = lax.all_gather(first, "col", axis=0, tiled=True, axis_index_groups=Y_GROUPS)
    second = exchange(jnp.broadcast_to(scaled[1][None], (NY, BLOCK, HALF)), "col", Y_GROUPS)
    second = jnp.broadcast_to(second[None], (NX, NY, BLOCK, HALF))
    second = exchange(second, "row", X_GROUPS).reshape(NX * NY, BLOCK, HALF)
    own, after, two, two_far, before = call_kernel(
        backward_kernel, place, entries, source, [first, second], [8, 8, 4, 4, 8]
    )
    two = jnp.concatenate([send_z(two, 2), send_z(two_far, -2)])
    near = (own + send_z(after, 1) + send_z(before, -1) + two).reshape(4, 2, BLOCK, HALF)
    is_own = (jnp.arange(4) == own_z // 4)[:, None, None, None]
    near = near + jnp.where(is_own, scaled[None], 0.0)
    halves = exchange(near.reshape(8, BLOCK, HALF), BOTH, Z_CORE)
    halves = jnp.sum(halves.reshape(4, 2, BLOCK, HALF), axis=0)
    gradient = jnp.concatenate([halves[0], halves[1]], axis=1)
    return (gradient, span_loss)


def solution(mesh):
    in_specs = (
        P(("row", "col"), None),
        P(("row", "col"), None, None, None),
        P(("row", "col"), None),
        P(("row", "col")),
        P(("row", "col"), None),
        P(("row", "col"), None),
        P(("row", "col"), None),
        P(("row", "col"), None),
    )
    out_specs = (P(("row", "col"), None), P(("row", "col")))
    return jax.shard_map(
        per_device, mesh=mesh, in_specs=in_specs, out_specs=out_specs, check_vma=False
    )
```

```python
import functools

import jax
import jax.numpy as jnp
from jax import lax
from jax.experimental import pallas as pl
from jax.experimental.pallas import tpu as pltpu
from jax.sharding import PartitionSpec as P

BLOCK = 128
NX = 4
NZ = 16
NY = 8
HALF = 128
SLOTS = 16
CB = 64
PAIRS = 64
ENTRIES = 2 * NX * SLOTS
EXTRA = 32
VMEM_LIMIT = 48 * 1024 * 1024

precise = lax.Precision.HIGHEST

BOTH = ("row", "col")
X_GROUPS = [[x * NZ + z for x in range(NX)] for z in range(NZ)]
Y_GROUPS = [[y * 2 + k for y in range(NY)] for k in range(2)]
X_CORE = [
    [(x * NZ + z) * 2 * NY + 2 * y + k for x in range(NX) for k in range(2)]
    for z in range(NZ)
    for y in range(NY)
]
Z_CORE = [
    [(x * NZ + 4 * a + b) * 2 * NY + 2 * y + k for a in range(4) for k in range(2)]
    for x in range(NX)
    for b in range(4)
    for y in range(NY)
]
CORE_SWAP = [(i, i ^ 1) for i in range(2 * NY)]


def send_z(values, step):
    pairs = [(x * NZ + z, x * NZ + (z + step) % NZ) for x in range(NX) for z in range(NZ)]
    return lax.ppermute(values, "row", pairs)


def swap_cores(values):
    return lax.ppermute(values, "col", CORE_SWAP)


def exchange(values, axis, groups):
    return lax.all_to_all(
        values, axis, split_axis=0, concat_axis=0, tiled=True, axis_index_groups=groups
    )


def split_bf16(values):
    high = values.astype(jnp.bfloat16)
    low = (values - high.astype(jnp.float32)).astype(jnp.bfloat16)
    return high, low


def product(left, right, contract):
    left_high, left_low = split_bf16(left)
    right_high, right_low = split_bf16(right)
    rows = jnp.concatenate([left_high, left_low, left_high], axis=contract)
    columns = jnp.concatenate([right_high, right_high, right_low], axis=0)
    dims = (((contract,), (0,)), ((), ()))
    return lax.dot_general(rows, columns, dims, preferred_element_type=jnp.float32)


def copy_block(entry, place, source_ref, blocks_ref, arrived, rows=slice(0, BLOCK)):
    window = pl.ds(rows.start, rows.stop - rows.start)
    block = source_ref.at[jnp.bitwise_and(entry, ENTRIES - 1), window]
    return pltpu.make_async_copy(block, blocks_ref.at[place, window], arrived.at[place])


def decode(entry, own_z):
    number, position = jnp.bitwise_and(entry, ENTRIES - 1), entry // ENTRIES
    z = jnp.bitwise_and(position, NZ - 1)
    near = jnp.bitwise_and(z - own_z, 3) * 8 + (z // 4) * 2
    near = near + jnp.bitwise_and(number // SLOTS, 1)
    return number // (2 * SLOTS), position // (2 * CB), near


def for_pairs(first, last, wait, compute, add):
    @pl.loop(0, (last - first + 1) // 2)
    def _(step):
        index = first + 2 * step
        both = index + 1 < last
        other = jnp.where(both, index + 1, index)
        wait(index)

        @pl.when(both)
        def _():
            wait(other)

        value, other_value = compute(index), compute(other)
        add(index, value)
        add(other, jnp.where(both, other_value, 0.0))


def forward_kernel(odd, place_ref, list_ref, source_ref, *refs):
    parts, out_ref, rows_ref, blocks_ref, arrived = refs[:5], refs[5], refs[6], refs[7], refs[8]
    own_z, even_end, end = place_ref[0], place_ref[1], place_ref[2]

    def copy(index, rows):
        return copy_block(list_ref[index], index, source_ref, blocks_ref, arrived, rows)

    top, rest, whole = slice(0, EXTRA), slice(EXTRA, BLOCK), slice(0, BLOCK)
    if odd:
        spans = [(even_end, end, rest, slice(0, BLOCK - EXTRA))]
    else:
        spans = [(0, even_end, whole, whole), (even_end, end, top, slice(BLOCK, BLOCK + EXTRA))]
    for first, last, rows, _ in spans:

        @pl.loop(first, last)
        def _(index):
            copy(index, rows).start()

    out_ref[...] = jnp.zeros_like(out_ref)
    start = 0
    for part in parts:
        rows_ref[pl.ds(start, part.shape[0])] = part[...]
        start += part.shape[0]

    for first, last, rows, out_rows in spans:

        def compute(index):
            _, _, near = decode(list_ref[index], own_z)
            return product(blocks_ref[index, rows], rows_ref[near], 1)

        def add(index, value):
            x, y, _ = decode(list_ref[index], own_z)
            out_ref[x * NY + y if odd else y * NX + x, out_rows] += value

        for_pairs(first, last, lambda index: copy(index, rows).wait(), compute, add)


def backward_kernel(place_ref, list_ref, source_ref, even_ref, odd_ref, *refs):
    outs, total_ref, blocks_ref, arrived, rows_ref, rows_arrived = refs[:5], *refs[5:]
    own_z, even_end, end = place_ref[0], place_ref[1], place_ref[2]

    def copy(index):
        return copy_block(list_ref[index], index, source_ref, blocks_ref, arrived)

    def copy_rows(index, source, place, source_rows, rows):
        return pltpu.make_async_copy(
            source.at[place, pl.ds(source_rows, rows.stop - rows.start)],
            rows_ref.at[index, pl.ds(rows.start, rows.stop - rows.start)],
            rows_arrived.at[index],
        )

    @pl.loop(0, even_end)
    def _(index):
        x, y, _ = decode(list_ref[index], own_z)
        copy(index).start()
        copy_rows(index, even_ref, y * NX + x, 0, slice(0, BLOCK)).start()

    @pl.loop(even_end, end)
    def _(index):
        x, y, _ = decode(list_ref[index], own_z)
        copy(index).start()
        copy_rows(index, even_ref, y * NX + x, BLOCK, slice(0, EXTRA)).start()
        copy_rows(index, odd_ref, x * NY + y, 0, slice(EXTRA, BLOCK)).start()

    total_ref[...] = jnp.zeros_like(total_ref)

    def wait(index):
        copy(index).wait()
        copy_rows(index, even_ref, 0, 0, slice(0, BLOCK)).wait()

    def compute(index):
        return product(blocks_ref[index], rows_ref[index], 0)

    def add(index, value):
        _, _, near = decode(list_ref[index], own_z)
        total_ref[near] += value

    for_pairs(0, end, wait, compute, add)
    start = 0
    for out in outs:
        out[...] = total_ref[pl.ds(start, out.shape[0])]
        start += out.shape[0]


def call_kernel(body, place, entries, source, arrays, out_shapes, in_place=True):
    whole = pl.BlockSpec(memory_space=pltpu.VMEM)
    scalars = pl.BlockSpec(memory_space=pltpu.SMEM)
    anywhere = pl.BlockSpec(memory_space=pl.ANY)
    copies = [
        pltpu.VMEM((ENTRIES, BLOCK, BLOCK), jnp.float32),
        pltpu.SemaphoreType.DMA((ENTRIES,)),
    ]
    return pl.pallas_call(
        body,
        out_shape=[jax.ShapeDtypeStruct((*shape, HALF), jnp.float32) for shape in out_shapes],
        in_specs=[scalars, scalars, anywhere] + [whole if in_place else anywhere] * len(arrays),
        out_specs=[whole] * len(out_shapes),
        scratch_shapes=[pltpu.VMEM((2 * NZ, BLOCK, HALF), jnp.float32)]
        + copies * (1 if in_place else 2),
        compiler_params=pltpu.CompilerParams(vmem_limit_bytes=VMEM_LIMIT),
    )(place, entries, source, *arrays)


def live_list(ids, own_x, own_z):
    numbers = jnp.arange(ENTRIES, dtype=jnp.int32)
    live = (ids >= 0) & (jnp.bitwise_and(ids, CB - 1) // NZ == own_x)
    odd = jnp.bitwise_and(ids // CB, 1) == 1
    even_live, odd_live = live & ~odd, live & odd
    before = numbers[None, :] < numbers[:, None]
    even_end = jnp.sum(even_live.astype(jnp.int32))
    rank = jnp.where(
        odd,
        even_end + jnp.sum((before & odd_live[None, :]).astype(jnp.int32), axis=1),
        jnp.sum((before & even_live[None, :]).astype(jnp.int32), axis=1),
    )
    hit = live[None, :] & (rank[None, :] == numbers[:, None])
    entries = jnp.sum(jnp.where(hit, (ids * ENTRIES + numbers)[None, :], 0), axis=1)
    return entries, jnp.stack([own_z, even_end, jnp.sum(live.astype(jnp.int32))])


def one_hot(indices, span_rows):
    return (indices[..., None] == jnp.arange(span_rows, dtype=jnp.int32)).astype(jnp.float32)


def per_device(table, blocks, block_ids, counts, users, positives, neg_index, popular):
    own_row = lax.axis_index("row")
    core = jnp.bitwise_and(lax.axis_index("col"), 1)
    own_z = jnp.bitwise_and(own_row, NZ - 1)
    source = lax.all_gather(blocks[0], BOTH, axis=0, tiled=True, axis_index_groups=X_CORE)

    halves = jnp.stack([table[:, :HALF], table[:, HALF:]])
    halves = jnp.broadcast_to(halves[None], (4, 2, BLOCK, HALF)).reshape(8, BLOCK, HALF)
    far = exchange(halves, BOTH, Z_CORE)
    span_table = lax.dynamic_slice_in_dim(far, own_z // 4 * 2, 2)
    parts = [far, send_z(far, -1), send_z(far[:4], -2), send_z(far[4:], 2), send_z(far, 1)]
    picks = jnp.stack([users[0], positives[0], jnp.take(positives[0], neg_index[0]), popular[0]])
    other_picks = swap_cores(picks)
    live = jnp.arange(SLOTS, dtype=jnp.int32) < counts[0]
    marked, _ = lax.optimization_barrier((jnp.where(live, block_ids[0], -1), far))
    ids = exchange(jnp.broadcast_to(marked[None], (2 * NX, SLOTS)), BOTH, X_CORE)
    entries, place = live_list(ids.reshape(-1), own_row // NZ, own_z)
    source, other_picks, entries, place, *parts = lax.optimization_barrier(
        (source, other_picks, entries, place, *parts)
    )
    even, odd = (functools.partial(forward_kernel, odd) for odd in (False, True))
    (first,) = call_kernel(even, place, entries, source, parts, [(NX * NY, BLOCK + EXTRA)])
    entries, first = lax.optimization_barrier((entries, first))
    (second,) = call_kernel(odd, place, entries, source, parts, [(NX * NY, BLOCK - EXTRA)])

    first = lax.psum_scatter(
        first, "col", scatter_dimension=0, tiled=True, axis_index_groups=Y_GROUPS
    )
    second = second.reshape(NX, NY * (BLOCK - EXTRA), HALF)
    second = jnp.sum(exchange(second, "row", X_GROUPS), axis=0)
    second = exchange(second.reshape(NY, BLOCK - EXTRA, HALF), "col", Y_GROUPS)
    second = jnp.sum(second, axis=0)
    first = jnp.sum(exchange(first, "row", X_GROUPS), axis=0)
    current = jnp.concatenate([first, second]).reshape(2, BLOCK, HALF)

    is_first = core == 0
    span_picks = [jnp.where(is_first, picks, other_picks), jnp.where(is_first, other_picks, picks)]
    final_rows = (span_table + current) / 2
    hot = one_hot(jnp.stack(span_picks), BLOCK)
    rows = jnp.einsum("hpij,hjd->hpid", hot, final_rows, precision=precise)
    user_rows, item_rows, batch_rows, popular_rows = (rows[:, i] for i in range(4))
    scores = jnp.stack(
        [
            jnp.sum(user_rows * item_rows, axis=-1),
            jnp.sum(user_rows * batch_rows, axis=-1),
            jnp.sum(user_rows * popular_rows, axis=-1),
        ],
        axis=1,
    )
    scores = scores + swap_cores(scores)
    first = scores[:, 1] - scores[:, 0]
    second = scores[:, 2] - scores[:, 0]
    losses = jax.nn.softplus(first) + jax.nn.softplus(second)
    span_losses = jnp.sum(losses, axis=1) / PAIRS
    span_loss = jnp.where(is_first, span_losses[0], span_losses[1]).reshape(1)
    pull_first = jax.nn.sigmoid(first)[..., None] / 2
    pull_second = jax.nn.sigmoid(second)[..., None] / 2
    pull_item = -(pull_first + pull_second)
    row_grads = jnp.stack(
        [
            pull_item * item_rows + pull_first * batch_rows + pull_second * popular_rows,
            pull_item * user_rows,
            pull_first * user_rows,
            pull_second * user_rows,
        ],
        axis=1,
    )
    scaled = jnp.einsum("hpij,hpid->hjd", hot, row_grads, precision=precise)

    all_rows = scaled.reshape(2 * BLOCK, HALF)
    first, second = all_rows[: BLOCK + EXTRA], all_rows[BLOCK + EXTRA :]
    first = exchange(jnp.broadcast_to(first[None], (NX, *first.shape)), "row", X_GROUPS)
    first = lax.all_gather(first, "col", axis=0, tiled=True, axis_index_groups=Y_GROUPS)
    second = exchange(jnp.broadcast_to(second[None], (NY, *second.shape)), "col", Y_GROUPS)
    second = second.reshape(NY * (BLOCK - EXTRA), HALF)
    second = exchange(jnp.broadcast_to(second[None], (NX, *second.shape)), "row", X_GROUPS)
    second = second.reshape(NX * NY, BLOCK - EXTRA, HALF)
    shapes = [(n, BLOCK) for n in (8, 8, 4, 4, 8)]
    own, after, two, two_far, before = call_kernel(
        backward_kernel, place, entries, source, [first, second], shapes, in_place=False
    )
    two = jnp.concatenate([send_z(two, 2), send_z(two_far, -2)])
    near = (own + send_z(after, 1) + send_z(before, -1) + two).reshape(4, 2, BLOCK, HALF)
    is_own = (jnp.arange(4) == own_z // 4)[:, None, None, None]
    near = near + jnp.where(is_own, scaled[None], 0.0)
    halves = exchange(near.reshape(8, BLOCK, HALF), BOTH, Z_CORE)
    halves = jnp.sum(halves.reshape(4, 2, BLOCK, HALF), axis=0)
    gradient = jnp.concatenate([halves[0], halves[1]], axis=1)
    return (gradient, span_loss)


def solution(mesh):
    in_specs = (
        P(("row", "col"), None),
        P(("row", "col"), None, None, None),
        P(("row", "col"), None),
        P(("row", "col")),
        P(("row", "col"), None),
        P(("row", "col"), None),
        P(("row", "col"), None),
        P(("row", "col"), None),
    )
    out_specs = (P(("row", "col"), None), P(("row", "col")))
    return jax.shard_map(
        per_device, mesh=mesh, in_specs=in_specs, out_specs=out_specs, check_vma=False
    )
```

```python
import functools

import jax
import jax.numpy as jnp
from jax import lax
from jax.experimental import pallas as pl
from jax.experimental.pallas import tpu as pltpu
from jax.sharding import PartitionSpec as P

BLOCK = 128
NX = 4
NZ = 16
NY = 8
HALF = 128
SLOTS = 16
CB = 64
PAIRS = 64
ENTRIES = 2 * NX * SLOTS
EXTRA = 16
VMEM_LIMIT = 48 * 1024 * 1024

precise = lax.Precision.HIGHEST

BOTH = ("row", "col")
X_GROUPS = [[x * NZ + z for x in range(NX)] for z in range(NZ)]
Y_GROUPS = [[y * 2 + k for y in range(NY)] for k in range(2)]
X_CORE = [
    [(x * NZ + z) * 2 * NY + 2 * y + k for x in range(NX) for k in range(2)]
    for z in range(NZ)
    for y in range(NY)
]
Z_CORE = [
    [(x * NZ + 4 * a + b) * 2 * NY + 2 * y + k for a in range(4) for k in range(2)]
    for x in range(NX)
    for b in range(4)
    for y in range(NY)
]
CORE_SWAP = [(i, i ^ 1) for i in range(2 * NY)]


def send_z(values, step):
    pairs = [(x * NZ + z, x * NZ + (z + step) % NZ) for x in range(NX) for z in range(NZ)]
    return lax.ppermute(values, "row", pairs)


def swap_cores(values):
    return lax.ppermute(values, "col", CORE_SWAP)


def exchange(values, axis, groups):
    return lax.all_to_all(
        values, axis, split_axis=0, concat_axis=0, tiled=True, axis_index_groups=groups
    )


def split_bf16(values):
    high = values.astype(jnp.bfloat16)
    low = (values - high.astype(jnp.float32)).astype(jnp.bfloat16)
    return high, low


def product(left, right, contract):
    left_high, left_low = split_bf16(left)
    right_high, right_low = split_bf16(right)
    rows = jnp.concatenate([left_high, left_low, left_high], axis=contract)
    columns = jnp.concatenate([right_high, right_high, right_low], axis=0)
    dims = (((contract,), (0,)), ((), ()))
    return lax.dot_general(rows, columns, dims, preferred_element_type=jnp.float32)


def copy_block(entry, place, source_ref, blocks_ref, arrived, rows=slice(0, BLOCK)):
    window = pl.ds(rows.start, rows.stop - rows.start)
    block = source_ref.at[jnp.bitwise_and(entry, ENTRIES - 1), window]
    return pltpu.make_async_copy(block, blocks_ref.at[place, window], arrived.at[place])


def decode(entry, own_z):
    number, position = jnp.bitwise_and(entry, ENTRIES - 1), entry // ENTRIES
    z = jnp.bitwise_and(position, NZ - 1)
    near = jnp.bitwise_and(z - own_z, 3) * 8 + (z // 4) * 2
    near = near + jnp.bitwise_and(number // SLOTS, 1)
    return number // (2 * SLOTS), position // (2 * CB), near


def for_pairs(first, last, wait, compute, add):
    @pl.loop(0, (last - first + 1) // 2)
    def _(step):
        index = first + 2 * step
        both = index + 1 < last
        other = jnp.where(both, index + 1, index)
        wait(index)

        @pl.when(both)
        def _():
            wait(other)

        value, other_value = compute(index), compute(other)
        add(index, value)
        add(other, jnp.where(both, other_value, 0.0))


def forward_kernel(odd, place_ref, list_ref, source_ref, *refs):
    parts, out_ref, rows_ref, blocks_ref, arrived = refs[:5], refs[5], refs[6], refs[7], refs[8]
    own_z, even_end, end = place_ref[0], place_ref[1], place_ref[2]

    def copy(index, rows):
        return copy_block(list_ref[index], index, source_ref, blocks_ref, arrived, rows)

    top, rest, whole = slice(0, EXTRA), slice(EXTRA, BLOCK), slice(0, BLOCK)
    if odd:
        spans = [(even_end, end, rest, slice(0, BLOCK - EXTRA))]
    else:
        spans = [(0, even_end, whole, whole), (even_end, end, top, slice(BLOCK, BLOCK + EXTRA))]
    for first, last, rows, _ in spans:

        @pl.loop(first, last)
        def _(index):
            copy(index, rows).start()

    out_ref[...] = jnp.zeros_like(out_ref)
    start = 0
    for part in parts:
        rows_ref[pl.ds(start, part.shape[0])] = part[...]
        start += part.shape[0]

    for first, last, rows, out_rows in spans:

        def compute(index):
            _, _, near = decode(list_ref[index], own_z)
            return product(blocks_ref[index, rows], rows_ref[near], 1)

        def add(index, value):
            x, y, _ = decode(list_ref[index], own_z)
            out_ref[y * NX + x, out_rows] += value

        for_pairs(first, last, lambda index: copy(index, rows).wait(), compute, add)


def backward_kernel(odd, place_ref, list_ref, source_ref, slab_ref, *refs):
    total_ref, blocks_ref, arrived, rows_ref, rows_arrived = refs[-5:]
    own_z, even_end, end = place_ref[0], place_ref[1], place_ref[2]

    def copy(index, rows):
        return copy_block(list_ref[index], index, source_ref, blocks_ref, arrived, rows)

    def copy_rows(index, rows, slab_start):
        x, y, _ = decode(list_ref[index], own_z)
        place = x * NY + y if odd else y * NX + x
        length = rows.stop - rows.start
        return pltpu.make_async_copy(
            slab_ref.at[place, pl.ds(slab_start, length)],
            rows_ref.at[index, pl.ds(rows.start, length)],
            rows_arrived.at[index],
        )

    if odd:
        spans = [(even_end, end, slice(EXTRA, BLOCK), 0)]
    else:
        spans = [(0, even_end, slice(0, BLOCK), 0), (even_end, end, slice(0, EXTRA), BLOCK)]
    for first, last, rows, slab_start in spans:

        @pl.loop(first, last)
        def _(index):
            copy(index, rows).start()
            copy_rows(index, rows, slab_start).start()

    if odd:
        total_ref[...] = jnp.zeros_like(total_ref)
    else:
        total_ref[...] = refs[0][...]

    for first, last, rows, slab_start in spans:

        def wait(index):
            copy(index, rows).wait()
            copy_rows(index, rows, slab_start).wait()

        def compute(index):
            return product(blocks_ref[index, rows], rows_ref[index, rows], 0)

        def add(index, value):
            _, _, near = decode(list_ref[index], own_z)
            total_ref[near] += value

        for_pairs(first, last, wait, compute, add)

    if not odd:
        start = 0
        for out in refs[1:-5]:
            out[...] = total_ref[pl.ds(start, out.shape[0])]
            start += out.shape[0]


def call_kernel(body, place, entries, source, arrays, specs, out_shapes, scratch):
    whole = pl.BlockSpec(memory_space=pltpu.VMEM)
    scalars = pl.BlockSpec(memory_space=pltpu.SMEM)
    anywhere = pl.BlockSpec(memory_space=pl.ANY)
    return pl.pallas_call(
        body,
        out_shape=[jax.ShapeDtypeStruct((*shape, HALF), jnp.float32) for shape in out_shapes],
        in_specs=[scalars, scalars, anywhere] + [anywhere if s else whole for s in specs],
        out_specs=[whole] * len(out_shapes),
        scratch_shapes=scratch,
        compiler_params=pltpu.CompilerParams(vmem_limit_bytes=VMEM_LIMIT),
    )(place, entries, source, *arrays)


def copies():
    return [
        pltpu.VMEM((ENTRIES, BLOCK, BLOCK), jnp.float32),
        pltpu.SemaphoreType.DMA((ENTRIES,)),
    ]


def forward_products(odd, place, entries, source, parts):
    rows = BLOCK - EXTRA if odd else BLOCK + EXTRA
    scratch = [pltpu.VMEM((2 * NZ, BLOCK, HALF), jnp.float32)] + copies()
    body = functools.partial(forward_kernel, odd)
    specs = [False] * len(parts)
    return call_kernel(body, place, entries, source, parts, specs, [(NX * NY, rows)], scratch)[0]


def backward_products(odd, place, entries, source, slab, total=None):
    body = functools.partial(backward_kernel, odd)
    if odd:
        shapes, arrays, scratch = [(2 * NZ, BLOCK)], [slab], []
    else:
        shapes, arrays = [(n, BLOCK) for n in (8, 8, 4, 4, 8)], [slab, total]
        scratch = [pltpu.VMEM((2 * NZ, BLOCK, HALF), jnp.float32)]
    scratch = scratch + copies() + copies()
    return call_kernel(body, place, entries, source, arrays, [True, False][: len(arrays)], shapes, scratch)


def live_list(ids, own_x, own_z):
    numbers = jnp.arange(ENTRIES, dtype=jnp.int32)
    live = (ids >= 0) & (jnp.bitwise_and(ids, CB - 1) // NZ == own_x)
    odd = jnp.bitwise_and(ids // CB, 1) == 1
    even_live, odd_live = live & ~odd, live & odd
    before = numbers[None, :] < numbers[:, None]
    even_end = jnp.sum(even_live.astype(jnp.int32))
    rank = jnp.where(
        odd,
        even_end + jnp.sum((before & odd_live[None, :]).astype(jnp.int32), axis=1),
        jnp.sum((before & even_live[None, :]).astype(jnp.int32), axis=1),
    )
    hit = live[None, :] & (rank[None, :] == numbers[:, None])
    entries = jnp.sum(jnp.where(hit, (ids * ENTRIES + numbers)[None, :], 0), axis=1)
    return entries, jnp.stack([own_z, even_end, jnp.sum(live.astype(jnp.int32))])


def one_hot(indices, span_rows):
    return (indices[..., None] == jnp.arange(span_rows, dtype=jnp.int32)).astype(jnp.float32)


def per_device(table, blocks, block_ids, counts, users, positives, neg_index, popular):
    own_row = lax.axis_index("row")
    core = jnp.bitwise_and(lax.axis_index("col"), 1)
    own_z = jnp.bitwise_and(own_row, NZ - 1)
    source = lax.all_gather(blocks[0], BOTH, axis=0, tiled=True, axis_index_groups=X_CORE)

    halves = jnp.stack([table[:, :HALF], table[:, HALF:]])
    halves = jnp.broadcast_to(halves[None], (4, 2, BLOCK, HALF)).reshape(8, BLOCK, HALF)
    far = exchange(halves, BOTH, Z_CORE)
    span_table = lax.dynamic_slice_in_dim(far, own_z // 4 * 2, 2)
    parts = [far, send_z(far, -1), send_z(far[:4], -2), send_z(far[4:], 2), send_z(far, 1)]
    picks = jnp.stack([users[0], positives[0], jnp.take(positives[0], neg_index[0]), popular[0]])
    other_picks = swap_cores(picks)
    live = jnp.arange(SLOTS, dtype=jnp.int32) < counts[0]
    marked, _ = lax.optimization_barrier((jnp.where(live, block_ids[0], -1), far))
    ids = exchange(jnp.broadcast_to(marked[None], (2 * NX, SLOTS)), BOTH, X_CORE)
    entries, place = live_list(ids.reshape(-1), own_row // NZ, own_z)
    source, other_picks, entries, place, *parts = lax.optimization_barrier(
        (source, other_picks, entries, place, *parts)
    )
    first = forward_products(False, place, entries, source, parts)
    entries, first = lax.optimization_barrier((entries, first))
    second = forward_products(True, place, entries, source, parts)

    first = lax.psum_scatter(
        first, "col", scatter_dimension=0, tiled=True, axis_index_groups=Y_GROUPS
    )
    second = second.reshape(NY, NX * (BLOCK - EXTRA), HALF)
    second = jnp.sum(exchange(second, "col", Y_GROUPS), axis=0)
    both = jnp.concatenate([first, second.reshape(NX, BLOCK - EXTRA, HALF)], axis=1)
    current = jnp.sum(exchange(both, "row", X_GROUPS), axis=0).reshape(2, BLOCK, HALF)

    is_first = core == 0
    span_picks = [jnp.where(is_first, picks, other_picks), jnp.where(is_first, other_picks, picks)]
    final_rows = (span_table + current) / 2
    hot = one_hot(jnp.stack(span_picks), BLOCK)
    rows = jnp.einsum("hpij,hjd->hpid", hot, final_rows, precision=precise)
    user_rows, item_rows, batch_rows, popular_rows = (rows[:, i] for i in range(4))
    scores = jnp.stack(
        [
            jnp.sum(user_rows * item_rows, axis=-1),
            jnp.sum(user_rows * batch_rows, axis=-1),
            jnp.sum(user_rows * popular_rows, axis=-1),
        ],
        axis=1,
    )
    scores = scores + swap_cores(scores)
    first = scores[:, 1] - scores[:, 0]
    second = scores[:, 2] - scores[:, 0]
    losses = jax.nn.softplus(first) + jax.nn.softplus(second)
    span_losses = jnp.sum(losses, axis=1) / PAIRS
    span_loss = jnp.where(is_first, span_losses[0], span_losses[1]).reshape(1)
    pull_first = jax.nn.sigmoid(first)[..., None] / 2
    pull_second = jax.nn.sigmoid(second)[..., None] / 2
    pull_item = -(pull_first + pull_second)
    row_grads = jnp.stack(
        [
            pull_item * item_rows + pull_first * batch_rows + pull_second * popular_rows,
            pull_item * user_rows,
            pull_first * user_rows,
            pull_second * user_rows,
        ],
        axis=1,
    )
    scaled = jnp.einsum("hpij,hpid->hjd", hot, row_grads, precision=precise)

    all_rows = scaled.reshape(2 * BLOCK, HALF)
    first, second = all_rows[: BLOCK + EXTRA], all_rows[BLOCK + EXTRA :]
    first = exchange(jnp.broadcast_to(first[None], (NX, *first.shape)), "row", X_GROUPS)
    first = lax.all_gather(first, "col", axis=0, tiled=True, axis_index_groups=Y_GROUPS)
    second = exchange(jnp.broadcast_to(second[None], (NY, *second.shape)), "col", Y_GROUPS)
    second = second.reshape(NY * (BLOCK - EXTRA), HALF)
    second = exchange(jnp.broadcast_to(second[None], (NX, *second.shape)), "row", X_GROUPS)
    second = second.reshape(NX * NY, BLOCK - EXTRA, HALF)
    (total,) = backward_products(True, place, entries, source, second)
    own, after, two, two_far, before = backward_products(
        False, place, entries, source, first, total
    )
    two = jnp.concatenate([send_z(two, 2), send_z(two_far, -2)])
    near = (own + send_z(after, 1) + send_z(before, -1) + two).reshape(4, 2, BLOCK, HALF)
    is_own = (jnp.arange(4) == own_z // 4)[:, None, None, None]
    near = near + jnp.where(is_own, scaled[None], 0.0)
    halves = exchange(near.reshape(8, BLOCK, HALF), BOTH, Z_CORE)
    halves = jnp.sum(halves.reshape(4, 2, BLOCK, HALF), axis=0)
    gradient = jnp.concatenate([halves[0], halves[1]], axis=1)
    return (gradient, span_loss)


def solution(mesh):
    in_specs = (
        P(("row", "col"), None),
        P(("row", "col"), None, None, None),
        P(("row", "col"), None),
        P(("row", "col")),
        P(("row", "col"), None),
        P(("row", "col"), None),
        P(("row", "col"), None),
        P(("row", "col"), None),
    )
    out_specs = (P(("row", "col"), None), P(("row", "col")))
    return jax.shard_map(
        per_device, mesh=mesh, in_specs=in_specs, out_specs=out_specs, check_vma=False
    )
```

```python
import functools

import jax
import jax.numpy as jnp
from jax import lax
from jax.experimental import pallas as pl
from jax.experimental.pallas import tpu as pltpu
from jax.sharding import PartitionSpec as P

BLOCK = 128
NX = 4
NZ = 16
NY = 8
HALF = 128
SLOTS = 16
CB = 64
PAIRS = 64
ENTRIES = 2 * NX * SLOTS
EXTRA = 48
EXTRA_BACK = 16
VMEM_LIMIT = 48 * 1024 * 1024

precise = lax.Precision.HIGHEST

BOTH = ("row", "col")
X_GROUPS = [[x * NZ + z for x in range(NX)] for z in range(NZ)]
Y_GROUPS = [[y * 2 + k for y in range(NY)] for k in range(2)]
X_CORE = [
    [(x * NZ + z) * 2 * NY + 2 * y + k for x in range(NX) for k in range(2)]
    for z in range(NZ)
    for y in range(NY)
]
Z_CORE = [
    [(x * NZ + 4 * a + b) * 2 * NY + 2 * y + k for a in range(4) for k in range(2)]
    for x in range(NX)
    for b in range(4)
    for y in range(NY)
]
CORE_SWAP = [(i, i ^ 1) for i in range(2 * NY)]


def send_z(values, step):
    pairs = [(x * NZ + z, x * NZ + (z + step) % NZ) for x in range(NX) for z in range(NZ)]
    return lax.ppermute(values, "row", pairs)


def swap_cores(values):
    return lax.ppermute(values, "col", CORE_SWAP)


def exchange(values, axis, groups):
    return lax.all_to_all(
        values, axis, split_axis=0, concat_axis=0, tiled=True, axis_index_groups=groups
    )


def split_bf16(values):
    high = values.astype(jnp.bfloat16)
    low = (values - high.astype(jnp.float32)).astype(jnp.bfloat16)
    return high, low


def product(left, right, contract):
    left_high, left_low = split_bf16(left)
    right_high, right_low = split_bf16(right)
    rows = jnp.concatenate([left_high, left_low, left_high], axis=contract)
    columns = jnp.concatenate([right_high, right_high, right_low], axis=0)
    dims = (((contract,), (0,)), ((), ()))
    return lax.dot_general(rows, columns, dims, preferred_element_type=jnp.float32)


def copy_block(entry, place, source_ref, blocks_ref, arrived, rows=slice(0, BLOCK)):
    window = pl.ds(rows.start, rows.stop - rows.start)
    block = source_ref.at[jnp.bitwise_and(entry, ENTRIES - 1), window]
    return pltpu.make_async_copy(block, blocks_ref.at[place, window], arrived.at[place])


def decode(entry, own_z):
    number, position = jnp.bitwise_and(entry, ENTRIES - 1), entry // ENTRIES
    z = jnp.bitwise_and(position, NZ - 1)
    near = jnp.bitwise_and(z - own_z, 3) * 8 + (z // 4) * 2
    near = near + jnp.bitwise_and(number // SLOTS, 1)
    return number // (2 * SLOTS), position // (2 * CB), near


def for_pairs(first, last, wait, compute, add):
    @pl.loop(0, (last - first + 1) // 2)
    def _(step):
        index = first + 2 * step
        both = index + 1 < last
        other = jnp.where(both, index + 1, index)
        wait(index)

        @pl.when(both)
        def _():
            wait(other)

        value, other_value = compute(index), compute(other)
        add(index, value)
        add(other, jnp.where(both, other_value, 0.0))


def forward_kernel(odd, place_ref, list_ref, source_ref, *refs):
    parts, out_ref, rows_ref, blocks_ref, arrived = refs[:5], refs[5], refs[6], refs[7], refs[8]
    own_z, even_end, end = place_ref[0], place_ref[1], place_ref[2]

    def copy(index, rows):
        return copy_block(list_ref[index], index, source_ref, blocks_ref, arrived, rows)

    top, rest, whole = slice(0, EXTRA), slice(EXTRA, BLOCK), slice(0, BLOCK)
    if odd:
        spans = [(even_end, end, rest, slice(0, BLOCK - EXTRA))]
    else:
        spans = [(0, even_end, whole, whole), (even_end, end, top, slice(BLOCK, BLOCK + EXTRA))]
    for first, last, rows, _ in spans:

        @pl.loop(first, last)
        def _(index):
            copy(index, rows).start()

    out_ref[...] = jnp.zeros_like(out_ref)
    start = 0
    for part in parts:
        rows_ref[pl.ds(start, part.shape[0])] = part[...]
        start += part.shape[0]

    for first, last, rows, out_rows in spans:

        def compute(index):
            _, _, near = decode(list_ref[index], own_z)
            return product(blocks_ref[index, rows], rows_ref[near], 1)

        def add(index, value):
            x, y, _ = decode(list_ref[index], own_z)
            out_ref[x * NY + y if odd else y * NX + x, out_rows] += value

        for_pairs(first, last, lambda index: copy(index, rows).wait(), compute, add)


def backward_kernel(place_ref, list_ref, source_ref, even_ref, odd_ref, *refs):
    outs, total_ref, blocks_ref, arrived, rows_ref, rows_arrived = refs[:5], *refs[5:]
    own_z, even_end, end = place_ref[0], place_ref[1], place_ref[2]

    def copy(index):
        return copy_block(list_ref[index], index, source_ref, blocks_ref, arrived)

    def copy_rows(index, source, place, source_rows, rows):
        return pltpu.make_async_copy(
            source.at[place, pl.ds(source_rows, rows.stop - rows.start)],
            rows_ref.at[index, pl.ds(rows.start, rows.stop - rows.start)],
            rows_arrived.at[index],
        )

    @pl.loop(0, even_end)
    def _(index):
        x, y, _ = decode(list_ref[index], own_z)
        copy(index).start()
        copy_rows(index, even_ref, y * NX + x, 0, slice(0, BLOCK)).start()

    @pl.loop(even_end, end)
    def _(index):
        x, y, _ = decode(list_ref[index], own_z)
        copy(index).start()
        copy_rows(index, even_ref, y * NX + x, BLOCK, slice(0, EXTRA_BACK)).start()
        copy_rows(index, odd_ref, x * NY + y, 0, slice(EXTRA_BACK, BLOCK)).start()

    total_ref[...] = jnp.zeros_like(total_ref)

    def wait(index):
        copy(index).wait()
        copy_rows(index, even_ref, 0, 0, slice(0, BLOCK)).wait()

    def compute(index):
        return product(blocks_ref[index], rows_ref[index], 0)

    def add(index, value):
        _, _, near = decode(list_ref[index], own_z)
        total_ref[near] += value

    for_pairs(0, end, wait, compute, add)
    start = 0
    for out in outs:
        out[...] = total_ref[pl.ds(start, out.shape[0])]
        start += out.shape[0]


def call_kernel(body, place, entries, source, arrays, out_shapes, in_place=True):
    whole = pl.BlockSpec(memory_space=pltpu.VMEM)
    scalars = pl.BlockSpec(memory_space=pltpu.SMEM)
    anywhere = pl.BlockSpec(memory_space=pl.ANY)
    copies = [
        pltpu.VMEM((ENTRIES, BLOCK, BLOCK), jnp.float32),
        pltpu.SemaphoreType.DMA((ENTRIES,)),
    ]
    return pl.pallas_call(
        body,
        out_shape=[jax.ShapeDtypeStruct((*shape, HALF), jnp.float32) for shape in out_shapes],
        in_specs=[scalars, scalars, anywhere] + [whole if in_place else anywhere] * len(arrays),
        out_specs=[whole] * len(out_shapes),
        scratch_shapes=[pltpu.VMEM((2 * NZ, BLOCK, HALF), jnp.float32)]
        + copies * (1 if in_place else 2),
        compiler_params=pltpu.CompilerParams(vmem_limit_bytes=VMEM_LIMIT),
    )(place, entries, source, *arrays)


def live_list(ids, own_x, own_z):
    numbers = jnp.arange(ENTRIES, dtype=jnp.int32)
    live = (ids >= 0) & (jnp.bitwise_and(ids, CB - 1) // NZ == own_x)
    odd = jnp.bitwise_and(ids // CB, 1) == 1
    even_live, odd_live = live & ~odd, live & odd
    before = numbers[None, :] < numbers[:, None]
    even_end = jnp.sum(even_live.astype(jnp.int32))
    rank = jnp.where(
        odd,
        even_end + jnp.sum((before & odd_live[None, :]).astype(jnp.int32), axis=1),
        jnp.sum((before & even_live[None, :]).astype(jnp.int32), axis=1),
    )
    hit = live[None, :] & (rank[None, :] == numbers[:, None])
    entries = jnp.sum(jnp.where(hit, (ids * ENTRIES + numbers)[None, :], 0), axis=1)
    return entries, jnp.stack([own_z, even_end, jnp.sum(live.astype(jnp.int32))])


def one_hot(indices, span_rows):
    return (indices[..., None] == jnp.arange(span_rows, dtype=jnp.int32)).astype(jnp.float32)


def per_device(table, blocks, block_ids, counts, users, positives, neg_index, popular):
    own_row = lax.axis_index("row")
    core = jnp.bitwise_and(lax.axis_index("col"), 1)
    own_z = jnp.bitwise_and(own_row, NZ - 1)
    source = lax.all_gather(blocks[0], BOTH, axis=0, tiled=True, axis_index_groups=X_CORE)

    halves = jnp.stack([table[:, :HALF], table[:, HALF:]])
    halves = jnp.broadcast_to(halves[None], (4, 2, BLOCK, HALF)).reshape(8, BLOCK, HALF)
    far = exchange(halves, BOTH, Z_CORE)
    span_table = lax.dynamic_slice_in_dim(far, own_z // 4 * 2, 2)
    parts = [far, send_z(far, -1), send_z(far[:4], -2), send_z(far[4:], 2), send_z(far, 1)]
    picks = jnp.stack([users[0], positives[0], jnp.take(positives[0], neg_index[0]), popular[0]])
    other_picks = swap_cores(picks)
    live = jnp.arange(SLOTS, dtype=jnp.int32) < counts[0]
    marked, _ = lax.optimization_barrier((jnp.where(live, block_ids[0], -1), far))
    ids = exchange(jnp.broadcast_to(marked[None], (2 * NX, SLOTS)), BOTH, X_CORE)
    entries, place = live_list(ids.reshape(-1), own_row // NZ, own_z)
    source, other_picks, entries, place, *parts = lax.optimization_barrier(
        (source, other_picks, entries, place, *parts)
    )
    even, odd = (functools.partial(forward_kernel, odd) for odd in (False, True))
    (first,) = call_kernel(even, place, entries, source, parts, [(NX * NY, BLOCK + EXTRA)])
    entries, first = lax.optimization_barrier((entries, first))
    (second,) = call_kernel(odd, place, entries, source, parts, [(NX * NY, BLOCK - EXTRA)])

    first = lax.psum_scatter(
        first, "col", scatter_dimension=0, tiled=True, axis_index_groups=Y_GROUPS
    )
    second = second.reshape(NX, NY * (BLOCK - EXTRA), HALF)
    second = jnp.sum(exchange(second, "row", X_GROUPS), axis=0)
    second = exchange(second.reshape(NY, BLOCK - EXTRA, HALF), "col", Y_GROUPS)
    second = jnp.sum(second, axis=0)
    first = jnp.sum(exchange(first, "row", X_GROUPS), axis=0)
    current = jnp.concatenate([first, second]).reshape(2, BLOCK, HALF)

    is_first = core == 0
    span_picks = [jnp.where(is_first, picks, other_picks), jnp.where(is_first, other_picks, picks)]
    final_rows = (span_table + current) / 2
    hot = one_hot(jnp.stack(span_picks), BLOCK)
    rows = jnp.einsum("hpij,hjd->hpid", hot, final_rows, precision=precise)
    user_rows, item_rows, batch_rows, popular_rows = (rows[:, i] for i in range(4))
    scores = jnp.stack(
        [
            jnp.sum(user_rows * item_rows, axis=-1),
            jnp.sum(user_rows * batch_rows, axis=-1),
            jnp.sum(user_rows * popular_rows, axis=-1),
        ],
        axis=1,
    )
    scores = scores + swap_cores(scores)
    first = scores[:, 1] - scores[:, 0]
    second = scores[:, 2] - scores[:, 0]
    losses = jax.nn.softplus(first) + jax.nn.softplus(second)
    span_losses = jnp.sum(losses, axis=1) / PAIRS
    span_loss = jnp.where(is_first, span_losses[0], span_losses[1]).reshape(1)
    pull_first = jax.nn.sigmoid(first)[..., None] / 2
    pull_second = jax.nn.sigmoid(second)[..., None] / 2
    pull_item = -(pull_first + pull_second)
    row_grads = jnp.stack(
        [
            pull_item * item_rows + pull_first * batch_rows + pull_second * popular_rows,
            pull_item * user_rows,
            pull_first * user_rows,
            pull_second * user_rows,
        ],
        axis=1,
    )
    scaled = jnp.einsum("hpij,hpid->hjd", hot, row_grads, precision=precise)

    all_rows = scaled.reshape(2 * BLOCK, HALF)
    first, second = all_rows[: BLOCK + EXTRA_BACK], all_rows[BLOCK + EXTRA_BACK :]
    first = exchange(jnp.broadcast_to(first[None], (NX, *first.shape)), "row", X_GROUPS)
    first = lax.all_gather(first, "col", axis=0, tiled=True, axis_index_groups=Y_GROUPS)
    second = exchange(jnp.broadcast_to(second[None], (NY, *second.shape)), "col", Y_GROUPS)
    second = second.reshape(NY * (BLOCK - EXTRA_BACK), HALF)
    second = exchange(jnp.broadcast_to(second[None], (NX, *second.shape)), "row", X_GROUPS)
    second = second.reshape(NX * NY, BLOCK - EXTRA_BACK, HALF)
    shapes = [(n, BLOCK) for n in (8, 8, 4, 4, 8)]
    own, after, two, two_far, before = call_kernel(
        backward_kernel, place, entries, source, [first, second], shapes, in_place=False
    )
    two = jnp.concatenate([send_z(two, 2), send_z(two_far, -2)])
    near = (own + send_z(after, 1) + send_z(before, -1) + two).reshape(4, 2, BLOCK, HALF)
    is_own = (jnp.arange(4) == own_z // 4)[:, None, None, None]
    near = near + jnp.where(is_own, scaled[None], 0.0)
    halves = exchange(near.reshape(8, BLOCK, HALF), BOTH, Z_CORE)
    halves = jnp.sum(halves.reshape(4, 2, BLOCK, HALF), axis=0)
    gradient = jnp.concatenate([halves[0], halves[1]], axis=1)
    return (gradient, span_loss)


def solution(mesh):
    in_specs = (
        P(("row", "col"), None),
        P(("row", "col"), None, None, None),
        P(("row", "col"), None),
        P(("row", "col")),
        P(("row", "col"), None),
        P(("row", "col"), None),
        P(("row", "col"), None),
        P(("row", "col"), None),
    )
    out_specs = (P(("row", "col"), None), P(("row", "col")))
    return jax.shard_map(
        per_device, mesh=mesh, in_specs=in_specs, out_specs=out_specs, check_vma=False
    )
```

```python
import functools

import jax
import jax.numpy as jnp
from jax import lax
from jax.experimental import pallas as pl
from jax.experimental.pallas import tpu as pltpu
from jax.sharding import PartitionSpec as P

BLOCK = 128
NX = 4
NZ = 16
NY = 8
HALF = 128
SLOTS = 16
CB = 64
PAIRS = 64
ENTRIES = 2 * NX * SLOTS
EXTRA = 48
EXTRA_BACK = 16
VMEM_LIMIT = 48 * 1024 * 1024

precise = lax.Precision.HIGHEST

BOTH = ("row", "col")
X_GROUPS = [[x * NZ + z for x in range(NX)] for z in range(NZ)]
Y_GROUPS = [[y * 2 + k for y in range(NY)] for k in range(2)]
X_CORE = [
    [(x * NZ + z) * 2 * NY + 2 * y + k for x in range(NX) for k in range(2)]
    for z in range(NZ)
    for y in range(NY)
]
Z_CORE = [
    [(x * NZ + 4 * a + b) * 2 * NY + 2 * y + k for a in range(4) for k in range(2)]
    for x in range(NX)
    for b in range(4)
    for y in range(NY)
]
CORE_SWAP = [(i, i ^ 1) for i in range(2 * NY)]


def send_x(values, step):
    pairs = [(x * NZ + z, ((x + step) % NX) * NZ + z) for x in range(NX) for z in range(NZ)]
    return lax.ppermute(values, "row", pairs)


def send_z(values, step):
    pairs = [(x * NZ + z, x * NZ + (z + step) % NZ) for x in range(NX) for z in range(NZ)]
    return lax.ppermute(values, "row", pairs)


def swap_cores(values):
    return lax.ppermute(values, "col", CORE_SWAP)


def exchange(values, axis, groups):
    return lax.all_to_all(
        values, axis, split_axis=0, concat_axis=0, tiled=True, axis_index_groups=groups
    )


def split_bf16(values):
    high = values.astype(jnp.bfloat16)
    low = (values - high.astype(jnp.float32)).astype(jnp.bfloat16)
    return high, low


def product(left, right, contract):
    left_high, left_low = split_bf16(left)
    right_high, right_low = split_bf16(right)
    rows = jnp.concatenate([left_high, left_low, left_high], axis=contract)
    columns = jnp.concatenate([right_high, right_high, right_low], axis=0)
    dims = (((contract,), (0,)), ((), ()))
    return lax.dot_general(rows, columns, dims, preferred_element_type=jnp.float32)


def copy_block(entry, place, source_ref, blocks_ref, arrived, rows=slice(0, BLOCK)):
    window = pl.ds(rows.start, rows.stop - rows.start)
    block = source_ref.at[jnp.bitwise_and(entry, ENTRIES - 1), window]
    return pltpu.make_async_copy(block, blocks_ref.at[place, window], arrived.at[place])


def decode(entry, own_z):
    number, position = jnp.bitwise_and(entry, ENTRIES - 1), entry // ENTRIES
    z = jnp.bitwise_and(position, NZ - 1)
    near = jnp.bitwise_and(z - own_z, 3) * 8 + (z // 4) * 2
    near = near + jnp.bitwise_and(number // SLOTS, 1)
    return number // (2 * SLOTS), position // (2 * CB), near


def for_pairs(first, last, wait, compute, add):
    @pl.loop(0, (last - first + 1) // 2)
    def _(step):
        index = first + 2 * step
        both = index + 1 < last
        other = jnp.where(both, index + 1, index)
        wait(index)

        @pl.when(both)
        def _():
            wait(other)

        value, other_value = compute(index), compute(other)
        add(index, value)
        add(other, jnp.where(both, other_value, 0.0))


def forward_kernel(odd, place_ref, list_ref, source_ref, *refs):
    parts, out_ref, rows_ref, blocks_ref, arrived = refs[:5], refs[5], refs[6], refs[7], refs[8]
    own_z, even_end, end = place_ref[0], place_ref[1], place_ref[2]

    def copy(index, rows):
        return copy_block(list_ref[index], index, source_ref, blocks_ref, arrived, rows)

    top, rest, whole = slice(0, EXTRA), slice(EXTRA, BLOCK), slice(0, BLOCK)
    if odd:
        spans = [(even_end, end, rest, slice(0, BLOCK - EXTRA))]
    else:
        spans = [(0, even_end, whole, whole), (even_end, end, top, slice(BLOCK, BLOCK + EXTRA))]
    for first, last, rows, _ in spans:

        @pl.loop(first, last)
        def _(index):
            copy(index, rows).start()

    out_ref[...] = jnp.zeros_like(out_ref)
    start = 0
    for part in parts:
        rows_ref[pl.ds(start, part.shape[0])] = part[...]
        start += part.shape[0]

    for first, last, rows, out_rows in spans:

        def compute(index):
            _, _, near = decode(list_ref[index], own_z)
            return product(blocks_ref[index, rows], rows_ref[near], 1)

        def add(index, value):
            x, y, _ = decode(list_ref[index], own_z)
            out_ref[x * NY + y if odd else y * NX + x, out_rows] += value

        for_pairs(first, last, lambda index: copy(index, rows).wait(), compute, add)


def backward_kernel(place_ref, list_ref, source_ref, even_ref, odd_ref, *refs):
    outs, total_ref, blocks_ref, arrived, rows_ref, rows_arrived = refs[:5], *refs[5:]
    own_z, even_end, end = place_ref[0], place_ref[1], place_ref[2]

    def copy(index):
        return copy_block(list_ref[index], index, source_ref, blocks_ref, arrived)

    def copy_rows(index, source, place, source_rows, rows):
        return pltpu.make_async_copy(
            source.at[place, pl.ds(source_rows, rows.stop - rows.start)],
            rows_ref.at[index, pl.ds(rows.start, rows.stop - rows.start)],
            rows_arrived.at[index],
        )

    @pl.loop(0, even_end)
    def _(index):
        x, y, _ = decode(list_ref[index], own_z)
        copy(index).start()
        copy_rows(index, even_ref, y * NX + x, 0, slice(0, BLOCK)).start()

    @pl.loop(even_end, end)
    def _(index):
        x, y, _ = decode(list_ref[index], own_z)
        copy(index).start()
        copy_rows(index, even_ref, y * NX + x, BLOCK, slice(0, EXTRA_BACK)).start()
        copy_rows(index, odd_ref, x * NY + y, 0, slice(EXTRA_BACK, BLOCK)).start()

    total_ref[...] = jnp.zeros_like(total_ref)

    def wait(index):
        copy(index).wait()
        copy_rows(index, even_ref, 0, 0, slice(0, BLOCK)).wait()

    def compute(index):
        return product(blocks_ref[index], rows_ref[index], 0)

    def add(index, value):
        _, _, near = decode(list_ref[index], own_z)
        total_ref[near] += value

    for_pairs(0, end, wait, compute, add)
    start = 0
    for out in outs:
        out[...] = total_ref[pl.ds(start, out.shape[0])]
        start += out.shape[0]


def call_kernel(body, place, entries, source, arrays, out_shapes, in_place=True):
    whole = pl.BlockSpec(memory_space=pltpu.VMEM)
    scalars = pl.BlockSpec(memory_space=pltpu.SMEM)
    anywhere = pl.BlockSpec(memory_space=pl.ANY)
    copies = [
        pltpu.VMEM((ENTRIES, BLOCK, BLOCK), jnp.float32),
        pltpu.SemaphoreType.DMA((ENTRIES,)),
    ]
    return pl.pallas_call(
        body,
        out_shape=[jax.ShapeDtypeStruct((*shape, HALF), jnp.float32) for shape in out_shapes],
        in_specs=[scalars, scalars, anywhere] + [whole if in_place else anywhere] * len(arrays),
        out_specs=[whole] * len(out_shapes),
        scratch_shapes=[pltpu.VMEM((2 * NZ, BLOCK, HALF), jnp.float32)]
        + copies * (1 if in_place else 2),
        compiler_params=pltpu.CompilerParams(vmem_limit_bytes=VMEM_LIMIT),
    )(place, entries, source, *arrays)


def halves_kernel(table_ref, out_ref):
    for index in range(out_ref.shape[0]):
        half = slice(index % 2 * HALF, (index % 2 + 1) * HALF)
        out_ref[index] = table_ref[:, half]


def repeat_halves(table):
    whole = pl.BlockSpec(memory_space=pltpu.VMEM)
    shape = jax.ShapeDtypeStruct((8, BLOCK, HALF), jnp.float32)
    return pl.pallas_call(halves_kernel, out_shape=shape, in_specs=[whole], out_specs=whole)(table)


def live_list(ids, own_x, own_z):
    numbers = jnp.arange(ENTRIES, dtype=jnp.int32)
    live = (ids >= 0) & (jnp.bitwise_and(ids, CB - 1) // NZ == own_x)
    odd = jnp.bitwise_and(ids // CB, 1) == 1
    even_live, odd_live = live & ~odd, live & odd
    before = numbers[None, :] < numbers[:, None]
    even_end = jnp.sum(even_live.astype(jnp.int32))
    rank = jnp.where(
        odd,
        even_end + jnp.sum((before & odd_live[None, :]).astype(jnp.int32), axis=1),
        jnp.sum((before & even_live[None, :]).astype(jnp.int32), axis=1),
    )
    hit = live[None, :] & (rank[None, :] == numbers[:, None])
    x = jnp.bitwise_and(own_x - numbers // (2 * SLOTS), NX - 1)
    gathered = x * (2 * SLOTS) + jnp.bitwise_and(numbers, 2 * SLOTS - 1)
    entries = jnp.sum(jnp.where(hit, (ids * ENTRIES + gathered)[None, :], 0), axis=1)
    return entries, jnp.stack([own_z, even_end, jnp.sum(live.astype(jnp.int32))])


def one_hot(indices, span_rows):
    return (indices[..., None] == jnp.arange(span_rows, dtype=jnp.int32)).astype(jnp.float32)


def per_device(table, blocks, block_ids, counts, users, positives, neg_index, popular):
    own_row = lax.axis_index("row")
    core = jnp.bitwise_and(lax.axis_index("col"), 1)
    own_z = jnp.bitwise_and(own_row, NZ - 1)
    source = lax.all_gather(blocks[0], BOTH, axis=0, tiled=True, axis_index_groups=X_CORE)

    far = exchange(repeat_halves(table), BOTH, Z_CORE)
    span_table = lax.dynamic_slice_in_dim(far, own_z // 4 * 2, 2)
    parts = [far, send_z(far, -1), send_z(far[:4], -2), send_z(far[4:], 2), send_z(far, 1)]
    live = jnp.arange(PAIRS, dtype=jnp.int32) < counts[0]
    marked = jnp.where(live, jnp.pad(block_ids[0], (0, PAIRS - SLOTS), constant_values=-1), -1)
    batch = jnp.take(positives[0], neg_index[0])
    picks = jnp.stack([users[0], positives[0], batch, popular[0], marked])
    other_picks = swap_cores(picks)
    is_first = core == 0
    span_picks = jnp.where(
        is_first, jnp.stack([picks, other_picks]), jnp.stack([other_picks, picks])
    )
    ids = span_picks[:, 4, :SLOTS]
    ids = jnp.stack([ids] + [send_x(ids, step) for step in range(1, NX)]).reshape(-1)
    entries, place = live_list(ids, own_row // NZ, own_z)
    source, span_picks, entries, place, *parts = lax.optimization_barrier(
        (source, span_picks, entries, place, *parts)
    )
    even, odd = (functools.partial(forward_kernel, odd) for odd in (False, True))
    (first,) = call_kernel(even, place, entries, source, parts, [(NX * NY, BLOCK + EXTRA)])
    entries, first = lax.optimization_barrier((entries, first))
    (second,) = call_kernel(odd, place, entries, source, parts, [(NX * NY, BLOCK - EXTRA)])

    first = lax.psum_scatter(
        first, "col", scatter_dimension=0, tiled=True, axis_index_groups=Y_GROUPS
    )
    second = second.reshape(NX, NY * (BLOCK - EXTRA), HALF)
    second = jnp.sum(exchange(second, "row", X_GROUPS), axis=0)
    second = exchange(second.reshape(NY, BLOCK - EXTRA, HALF), "col", Y_GROUPS)
    second = jnp.sum(second, axis=0)
    first = jnp.sum(exchange(first, "row", X_GROUPS), axis=0)
    current = jnp.concatenate([first, second]).reshape(2, BLOCK, HALF)

    final_rows = (span_table + current) / 2
    hot = one_hot(span_picks[:, :4], BLOCK)
    rows = jnp.einsum("hpij,hjd->hpid", hot, final_rows, precision=precise)
    user_rows, item_rows, batch_rows, popular_rows = (rows[:, i] for i in range(4))
    scores = jnp.stack(
        [
            jnp.sum(user_rows * item_rows, axis=-1),
            jnp.sum(user_rows * batch_rows, axis=-1),
            jnp.sum(user_rows * popular_rows, axis=-1),
        ],
        axis=1,
    )
    scores = scores + swap_cores(scores)
    first = scores[:, 1] - scores[:, 0]
    second = scores[:, 2] - scores[:, 0]
    losses = jax.nn.softplus(first) + jax.nn.softplus(second)
    span_losses = jnp.sum(losses, axis=1) / PAIRS
    span_loss = jnp.where(is_first, span_losses[0], span_losses[1]).reshape(1)
    pull_first = jax.nn.sigmoid(first)[..., None] / 2
    pull_second = jax.nn.sigmoid(second)[..., None] / 2
    pull_item = -(pull_first + pull_second)
    row_grads = jnp.stack(
        [
            pull_item * item_rows + pull_first * batch_rows + pull_second * popular_rows,
            pull_item * user_rows,
            pull_first * user_rows,
            pull_second * user_rows,
        ],
        axis=1,
    )
    scaled = jnp.einsum("hpij,hpid->hjd", hot, row_grads, precision=precise)

    all_rows = scaled.reshape(2 * BLOCK, HALF)
    first, second = all_rows[: BLOCK + EXTRA_BACK], all_rows[BLOCK + EXTRA_BACK :]
    first = exchange(jnp.broadcast_to(first[None], (NX, *first.shape)), "row", X_GROUPS)
    first = lax.all_gather(first, "col", axis=0, tiled=True, axis_index_groups=Y_GROUPS)
    second = exchange(jnp.broadcast_to(second[None], (NY, *second.shape)), "col", Y_GROUPS)
    second = second.reshape(NY * (BLOCK - EXTRA_BACK), HALF)
    second = exchange(jnp.broadcast_to(second[None], (NX, *second.shape)), "row", X_GROUPS)
    second = second.reshape(NX * NY, BLOCK - EXTRA_BACK, HALF)
    shapes = [(n, BLOCK) for n in (8, 8, 4, 4, 8)]
    own, after, two, two_far, before = call_kernel(
        backward_kernel, place, entries, source, [first, second], shapes, in_place=False
    )
    two = jnp.concatenate([send_z(two, 2), send_z(two_far, -2)])
    near = (own + send_z(after, 1) + send_z(before, -1) + two).reshape(4, 2, BLOCK, HALF)
    is_own = (jnp.arange(4) == own_z // 4)[:, None, None, None]
    near = near + jnp.where(is_own, scaled[None], 0.0)
    halves = exchange(near.reshape(8, BLOCK, HALF), BOTH, Z_CORE)
    halves = jnp.sum(halves.reshape(4, 2, BLOCK, HALF), axis=0)
    gradient = jnp.concatenate([halves[0], halves[1]], axis=1)
    return (gradient, span_loss)


def solution(mesh):
    in_specs = (
        P(("row", "col"), None),
        P(("row", "col"), None, None, None),
        P(("row", "col"), None),
        P(("row", "col")),
        P(("row", "col"), None),
        P(("row", "col"), None),
        P(("row", "col"), None),
        P(("row", "col"), None),
    )
    out_specs = (P(("row", "col"), None), P(("row", "col")))
    return jax.shard_map(
        per_device, mesh=mesh, in_specs=in_specs, out_specs=out_specs, check_vma=False
    )
```

```python
import functools

import jax
import jax.numpy as jnp
from jax import lax
from jax.experimental import pallas as pl
from jax.experimental.pallas import tpu as pltpu
from jax.sharding import PartitionSpec as P

BLOCK = 128
NX = 4
NZ = 16
NY = 8
HALF = 128
SLOTS = 16
CB = 64
PAIRS = 64
ENTRIES = 2 * NX * SLOTS
EXTRA = 32
EXTRA_BACK = 16
GROUP = 4
VMEM_LIMIT = 48 * 1024 * 1024

precise = lax.Precision.HIGHEST

BOTH = ("row", "col")
X_GROUPS = [[x * NZ + z for x in range(NX)] for z in range(NZ)]
Y_GROUPS = [[y * 2 + k for y in range(NY)] for k in range(2)]
X_CORE = [
    [(x * NZ + z) * 2 * NY + 2 * y + k for x in range(NX) for k in range(2)]
    for z in range(NZ)
    for y in range(NY)
]
Z_CORE = [
    [(x * NZ + 4 * a + b) * 2 * NY + 2 * y + k for a in range(4) for k in range(2)]
    for x in range(NX)
    for b in range(4)
    for y in range(NY)
]
CORE_SWAP = [(i, i ^ 1) for i in range(2 * NY)]


def send_x(values, step):
    pairs = [(x * NZ + z, ((x + step) % NX) * NZ + z) for x in range(NX) for z in range(NZ)]
    return lax.ppermute(values, "row", pairs)


def send_z(values, step):
    pairs = [(x * NZ + z, x * NZ + (z + step) % NZ) for x in range(NX) for z in range(NZ)]
    return lax.ppermute(values, "row", pairs)


def swap_cores(values):
    return lax.ppermute(values, "col", CORE_SWAP)


def exchange(values, axis, groups):
    return lax.all_to_all(
        values, axis, split_axis=0, concat_axis=0, tiled=True, axis_index_groups=groups
    )


def split_bf16(values):
    high = values.astype(jnp.bfloat16)
    low = (values - high.astype(jnp.float32)).astype(jnp.bfloat16)
    return high, low


def product(left, right, contract):
    left_high, left_low = split_bf16(left)
    right_high, right_low = split_bf16(right)
    rows = jnp.concatenate([left_high, left_low, left_high], axis=contract)
    columns = jnp.concatenate([right_high, right_high, right_low], axis=0)
    dims = (((contract,), (0,)), ((), ()))
    return lax.dot_general(rows, columns, dims, preferred_element_type=jnp.float32)


def copy_block(entry, place, source_ref, blocks_ref, arrived, rows=slice(0, BLOCK)):
    window = pl.ds(rows.start, rows.stop - rows.start)
    block = source_ref.at[jnp.bitwise_and(entry, ENTRIES - 1), window]
    return pltpu.make_async_copy(block, blocks_ref.at[place, window], arrived.at[place])


def decode(entry, own_z):
    number, position = jnp.bitwise_and(entry, ENTRIES - 1), entry // ENTRIES
    z = jnp.bitwise_and(position, NZ - 1)
    near = jnp.bitwise_and(z - own_z, 3) * 8 + (z // 4) * 2
    near = near + jnp.bitwise_and(number // SLOTS, 1)
    return number // (2 * SLOTS), position // (2 * CB), near


def for_groups(first, last, wait, compute, add):
    @pl.loop(0, (last - first + GROUP - 1) // GROUP)
    def _(step):
        start = first + GROUP * step
        wait(start)
        for index in range(1, GROUP):

            @pl.when(start + index < last)
            def _():
                wait(start + index)

        places = [jnp.minimum(start + index, last - 1) for index in range(GROUP)]
        values = [compute(place) for place in places]
        for index, (place, value) in enumerate(zip(places, values)):
            add(place, value if index == 0 else jnp.where(start + index < last, value, 0.0))


def forward_kernel(odd, place_ref, list_ref, source_ref, *refs):
    parts, out_ref, rows_ref, blocks_ref, arrived = refs[:5], refs[5], refs[6], refs[7], refs[8]
    own_z, even_end, end = place_ref[0], place_ref[1], place_ref[2]

    def copy(index, rows):
        return copy_block(list_ref[index], index, source_ref, blocks_ref, arrived, rows)

    top, rest, whole = slice(0, EXTRA), slice(EXTRA, BLOCK), slice(0, BLOCK)
    if odd:
        spans = [(even_end, end, rest, slice(0, BLOCK - EXTRA))]
    else:
        spans = [(0, even_end, whole, whole), (even_end, end, top, slice(BLOCK, BLOCK + EXTRA))]
    for first, last, rows, _ in spans:

        @pl.loop(first, last)
        def _(index):
            copy(index, rows).start()

    out_ref[...] = jnp.zeros_like(out_ref)
    start = 0
    for part in parts:
        rows_ref[pl.ds(start, part.shape[0])] = part[...]
        start += part.shape[0]

    for first, last, rows, out_rows in spans:

        def compute(index):
            _, _, near = decode(list_ref[index], own_z)
            return product(blocks_ref[index, rows], rows_ref[near], 1)

        def add(index, value):
            x, y, _ = decode(list_ref[index], own_z)
            out_ref[x * NY + y if odd else y * NX + x, out_rows] += value

        for_groups(first, last, lambda index: copy(index, rows).wait(), compute, add)


def backward_kernel(place_ref, list_ref, source_ref, even_ref, odd_ref, *refs):
    outs, total_ref, blocks_ref, arrived, rows_ref, rows_arrived = refs[:5], *refs[5:]
    own_z, even_end, end = place_ref[0], place_ref[1], place_ref[2]

    def copy(index):
        return copy_block(list_ref[index], index, source_ref, blocks_ref, arrived)

    def copy_rows(index, source, place, source_rows, rows):
        return pltpu.make_async_copy(
            source.at[place, pl.ds(source_rows, rows.stop - rows.start)],
            rows_ref.at[index, pl.ds(rows.start, rows.stop - rows.start)],
            rows_arrived.at[index],
        )

    @pl.loop(0, even_end)
    def _(index):
        x, y, _ = decode(list_ref[index], own_z)
        copy(index).start()
        copy_rows(index, even_ref, y * NX + x, 0, slice(0, BLOCK)).start()

    @pl.loop(even_end, end)
    def _(index):
        x, y, _ = decode(list_ref[index], own_z)
        copy(index).start()
        copy_rows(index, even_ref, y * NX + x, BLOCK, slice(0, EXTRA_BACK)).start()
        copy_rows(index, odd_ref, x * NY + y, 0, slice(EXTRA_BACK, BLOCK)).start()

    total_ref[...] = jnp.zeros_like(total_ref)

    def wait(index):
        copy(index).wait()
        copy_rows(index, even_ref, 0, 0, slice(0, BLOCK)).wait()

    def compute(index):
        return product(blocks_ref[index], rows_ref[index], 0)

    def add(index, value):
        _, _, near = decode(list_ref[index], own_z)
        total_ref[near] += value

    for_groups(0, end, wait, compute, add)
    start = 0
    for out in outs:
        out[...] = total_ref[pl.ds(start, out.shape[0])]
        start += out.shape[0]


def call_kernel(body, place, entries, source, arrays, out_shapes, in_place=True):
    whole = pl.BlockSpec(memory_space=pltpu.VMEM)
    scalars = pl.BlockSpec(memory_space=pltpu.SMEM)
    anywhere = pl.BlockSpec(memory_space=pl.ANY)
    copies = [
        pltpu.VMEM((ENTRIES, BLOCK, BLOCK), jnp.float32),
        pltpu.SemaphoreType.DMA((ENTRIES,)),
    ]
    return pl.pallas_call(
        body,
        out_shape=[jax.ShapeDtypeStruct((*shape, HALF), jnp.float32) for shape in out_shapes],
        in_specs=[scalars, scalars, anywhere] + [whole if in_place else anywhere] * len(arrays),
        out_specs=[whole] * len(out_shapes),
        scratch_shapes=[pltpu.VMEM((2 * NZ, BLOCK, HALF), jnp.float32)]
        + copies * (1 if in_place else 2),
        compiler_params=pltpu.CompilerParams(vmem_limit_bytes=VMEM_LIMIT),
    )(place, entries, source, *arrays)


def halves_kernel(table_ref, out_ref):
    for index in range(out_ref.shape[0]):
        half = slice(index % 2 * HALF, (index % 2 + 1) * HALF)
        out_ref[index] = table_ref[:, half]


def repeat_halves(table):
    whole = pl.BlockSpec(memory_space=pltpu.VMEM)
    shape = jax.ShapeDtypeStruct((8, BLOCK, HALF), jnp.float32)
    return pl.pallas_call(halves_kernel, out_shape=shape, in_specs=[whole], out_specs=whole)(table)


def live_list(ids, own_x, own_z):
    numbers = jnp.arange(ENTRIES, dtype=jnp.int32)
    live = (ids >= 0) & (jnp.bitwise_and(ids, CB - 1) // NZ == own_x)
    odd = jnp.bitwise_and(ids // CB, 1) == 1
    even_live, odd_live = live & ~odd, live & odd
    before = numbers[None, :] < numbers[:, None]
    even_end = jnp.sum(even_live.astype(jnp.int32))
    rank = jnp.where(
        odd,
        even_end + jnp.sum((before & odd_live[None, :]).astype(jnp.int32), axis=1),
        jnp.sum((before & even_live[None, :]).astype(jnp.int32), axis=1),
    )
    hit = live[None, :] & (rank[None, :] == numbers[:, None])
    x = jnp.bitwise_and(own_x - numbers // (2 * SLOTS), NX - 1)
    gathered = x * (2 * SLOTS) + jnp.bitwise_and(numbers, 2 * SLOTS - 1)
    entries = jnp.sum(jnp.where(hit, (ids * ENTRIES + gathered)[None, :], 0), axis=1)
    return entries, jnp.stack([own_z, even_end, jnp.sum(live.astype(jnp.int32))])


def one_hot(indices, span_rows):
    return (indices[..., None] == jnp.arange(span_rows, dtype=jnp.int32)).astype(jnp.float32)


def per_device(table, blocks, block_ids, counts, users, positives, neg_index, popular):
    own_row = lax.axis_index("row")
    core = jnp.bitwise_and(lax.axis_index("col"), 1)
    own_z = jnp.bitwise_and(own_row, NZ - 1)
    source = lax.all_gather(blocks[0], BOTH, axis=0, tiled=True, axis_index_groups=X_CORE)

    far = exchange(repeat_halves(table), BOTH, Z_CORE)
    span_table = lax.dynamic_slice_in_dim(far, own_z // 4 * 2, 2)
    parts = [far, send_z(far, -1), send_z(far[:4], -2), send_z(far[4:], 2), send_z(far, 1)]
    live = jnp.arange(PAIRS, dtype=jnp.int32) < counts[0]
    marked = jnp.where(live, jnp.pad(block_ids[0], (0, PAIRS - SLOTS), constant_values=-1), -1)
    batch = jnp.take(positives[0], neg_index[0])
    picks = jnp.stack([users[0], positives[0], batch, popular[0], marked])
    other_picks = swap_cores(picks)
    is_first = core == 0
    span_picks = jnp.where(
        is_first, jnp.stack([picks, other_picks]), jnp.stack([other_picks, picks])
    )
    ids = span_picks[:, 4, :SLOTS]
    ids = jnp.stack([ids] + [send_x(ids, step) for step in range(1, NX)]).reshape(-1)
    entries, place = live_list(ids, own_row // NZ, own_z)
    source, span_picks, entries, place, *parts = lax.optimization_barrier(
        (source, span_picks, entries, place, *parts)
    )
    even, odd = (functools.partial(forward_kernel, odd) for odd in (False, True))
    (first,) = call_kernel(even, place, entries, source, parts, [(NX * NY, BLOCK + EXTRA)])
    entries, first = lax.optimization_barrier((entries, first))
    (second,) = call_kernel(odd, place, entries, source, parts, [(NX * NY, BLOCK - EXTRA)])

    first = lax.psum_scatter(
        first, "col", scatter_dimension=0, tiled=True, axis_index_groups=Y_GROUPS
    )
    second = second.reshape(NX, NY * (BLOCK - EXTRA), HALF)
    second = jnp.sum(exchange(second, "row", X_GROUPS), axis=0)
    second = exchange(second.reshape(NY, BLOCK - EXTRA, HALF), "col", Y_GROUPS)
    second = jnp.sum(second, axis=0)
    first = jnp.sum(exchange(first, "row", X_GROUPS), axis=0)
    current = jnp.concatenate([first, second]).reshape(2, BLOCK, HALF)

    final_rows = (span_table + current) / 2
    hot = one_hot(span_picks[:, :4], BLOCK)
    rows = jnp.einsum("hpij,hjd->hpid", hot, final_rows, precision=precise)
    user_rows, item_rows, batch_rows, popular_rows = (rows[:, i] for i in range(4))
    scores = jnp.stack(
        [
            jnp.sum(user_rows * item_rows, axis=-1),
            jnp.sum(user_rows * batch_rows, axis=-1),
            jnp.sum(user_rows * popular_rows, axis=-1),
        ],
        axis=1,
    )
    scores = scores + swap_cores(scores)
    first = scores[:, 1] - scores[:, 0]
    second = scores[:, 2] - scores[:, 0]
    losses = jax.nn.softplus(first) + jax.nn.softplus(second)
    span_losses = jnp.sum(losses, axis=1) / PAIRS
    span_loss = jnp.where(is_first, span_losses[0], span_losses[1]).reshape(1)
    pull_first = jax.nn.sigmoid(first)[..., None] / 2
    pull_second = jax.nn.sigmoid(second)[..., None] / 2
    pull_item = -(pull_first + pull_second)
    row_grads = jnp.stack(
        [
            pull_item * item_rows + pull_first * batch_rows + pull_second * popular_rows,
            pull_item * user_rows,
            pull_first * user_rows,
            pull_second * user_rows,
        ],
        axis=1,
    )
    scaled = jnp.einsum("hpij,hpid->hjd", hot, row_grads, precision=precise)

    all_rows = scaled.reshape(2 * BLOCK, HALF)
    first, second = all_rows[: BLOCK + EXTRA_BACK], all_rows[BLOCK + EXTRA_BACK :]
    first = exchange(jnp.broadcast_to(first[None], (NX, *first.shape)), "row", X_GROUPS)
    first = lax.all_gather(first, "col", axis=0, tiled=True, axis_index_groups=Y_GROUPS)
    second = exchange(jnp.broadcast_to(second[None], (NY, *second.shape)), "col", Y_GROUPS)
    second = second.reshape(NY * (BLOCK - EXTRA_BACK), HALF)
    second = exchange(jnp.broadcast_to(second[None], (NX, *second.shape)), "row", X_GROUPS)
    second = second.reshape(NX * NY, BLOCK - EXTRA_BACK, HALF)
    shapes = [(n, BLOCK) for n in (8, 8, 4, 4, 8)]
    own, after, two, two_far, before = call_kernel(
        backward_kernel, place, entries, source, [first, second], shapes, in_place=False
    )
    two = jnp.concatenate([send_z(two, 2), send_z(two_far, -2)])
    near = (own + send_z(after, 1) + send_z(before, -1) + two).reshape(4, 2, BLOCK, HALF)
    is_own = (jnp.arange(4) == own_z // 4)[:, None, None, None]
    near = near + jnp.where(is_own, scaled[None], 0.0)
    halves = exchange(near.reshape(8, BLOCK, HALF), BOTH, Z_CORE)
    halves = jnp.sum(halves.reshape(4, 2, BLOCK, HALF), axis=0)
    gradient = jnp.concatenate([halves[0], halves[1]], axis=1)
    return (gradient, span_loss)


def solution(mesh):
    in_specs = (
        P(("row", "col"), None),
        P(("row", "col"), None, None, None),
        P(("row", "col"), None),
        P(("row", "col")),
        P(("row", "col"), None),
        P(("row", "col"), None),
        P(("row", "col"), None),
        P(("row", "col"), None),
    )
    out_specs = (P(("row", "col"), None), P(("row", "col")))
    return jax.shard_map(
        per_device, mesh=mesh, in_specs=in_specs, out_specs=out_specs, check_vma=False
    )
```

```python
import functools

import jax
import jax.numpy as jnp
from jax import lax
from jax.experimental import pallas as pl
from jax.experimental.pallas import tpu as pltpu
from jax.sharding import PartitionSpec as P

BLOCK = 128
NX = 4
NZ = 16
NY = 8
HALF = 128
SLOTS = 16
CB = 64
PAIRS = 64
ENTRIES = 2 * NX * SLOTS
EXTRA = 32
EXTRA_BACK = 16
GROUP = 8
VMEM_LIMIT = 48 * 1024 * 1024

precise = lax.Precision.HIGHEST

BOTH = ("row", "col")
X_GROUPS = [[x * NZ + z for x in range(NX)] for z in range(NZ)]
Y_GROUPS = [[y * 2 + k for y in range(NY)] for k in range(2)]
X_CORE = [
    [(x * NZ + z) * 2 * NY + 2 * y + k for x in range(NX) for k in range(2)]
    for z in range(NZ)
    for y in range(NY)
]
Z_CORE = [
    [(x * NZ + 4 * a + b) * 2 * NY + 2 * y + k for a in range(4) for k in range(2)]
    for x in range(NX)
    for b in range(4)
    for y in range(NY)
]
CORE_SWAP = [(i, i ^ 1) for i in range(2 * NY)]


def send_x(values, step):
    pairs = [(x * NZ + z, ((x + step) % NX) * NZ + z) for x in range(NX) for z in range(NZ)]
    return lax.ppermute(values, "row", pairs)


def send_z(values, step):
    pairs = [(x * NZ + z, x * NZ + (z + step) % NZ) for x in range(NX) for z in range(NZ)]
    return lax.ppermute(values, "row", pairs)


def swap_cores(values):
    return lax.ppermute(values, "col", CORE_SWAP)


def exchange(values, axis, groups):
    return lax.all_to_all(
        values, axis, split_axis=0, concat_axis=0, tiled=True, axis_index_groups=groups
    )


def split_bf16(values):
    high = values.astype(jnp.bfloat16)
    low = (values - high.astype(jnp.float32)).astype(jnp.bfloat16)
    return high, low


def product(left, right, contract):
    left_high, left_low = split_bf16(left)
    right_high, right_low = split_bf16(right)
    rows = jnp.concatenate([left_high, left_low, left_high], axis=contract)
    columns = jnp.concatenate([right_high, right_high, right_low], axis=0)
    dims = (((contract,), (0,)), ((), ()))
    return lax.dot_general(rows, columns, dims, preferred_element_type=jnp.float32)


def copy_block(entry, place, source_ref, blocks_ref, arrived, rows=slice(0, BLOCK)):
    window = pl.ds(rows.start, rows.stop - rows.start)
    block = source_ref.at[jnp.bitwise_and(entry, ENTRIES - 1), window]
    return pltpu.make_async_copy(block, blocks_ref.at[place, window], arrived.at[place])


def decode(entry, own_z):
    number, position = jnp.bitwise_and(entry, ENTRIES - 1), entry // ENTRIES
    z = jnp.bitwise_and(position, NZ - 1)
    near = jnp.bitwise_and(z - own_z, 3) * 8 + (z // 4) * 2
    near = near + jnp.bitwise_and(number // SLOTS, 1)
    return number // (2 * SLOTS), position // (2 * CB), near


def for_groups(first, last, wait, compute, add):
    @pl.loop(0, (last - first + GROUP - 1) // GROUP)
    def _(step):
        start = first + GROUP * step
        wait(start)
        for index in range(1, GROUP):

            @pl.when(start + index < last)
            def _():
                wait(start + index)

        places = [jnp.minimum(start + index, last - 1) for index in range(GROUP)]
        values = [compute(place) for place in places]
        for index, (place, value) in enumerate(zip(places, values)):
            add(place, value if index == 0 else jnp.where(start + index < last, value, 0.0))


def forward_kernel(odd, place_ref, list_ref, source_ref, *refs):
    parts, out_ref, rows_ref, blocks_ref, arrived = refs[:5], refs[5], refs[6], refs[7], refs[8]
    own_z, even_end, end = place_ref[0], place_ref[1], place_ref[2]

    def copy(index, rows):
        return copy_block(list_ref[index], index, source_ref, blocks_ref, arrived, rows)

    top, rest, whole = slice(0, EXTRA), slice(EXTRA, BLOCK), slice(0, BLOCK)
    if odd:
        spans = [(even_end, end, rest, slice(0, BLOCK - EXTRA))]
    else:
        spans = [(0, even_end, whole, whole), (even_end, end, top, slice(BLOCK, BLOCK + EXTRA))]
    for first, last, rows, _ in spans:

        @pl.loop(first, last)
        def _(index):
            copy(index, rows).start()

    out_ref[...] = jnp.zeros_like(out_ref)
    start = 0
    for part in parts:
        rows_ref[pl.ds(start, part.shape[0])] = part[...]
        start += part.shape[0]

    for first, last, rows, out_rows in spans:

        def compute(index):
            _, _, near = decode(list_ref[index], own_z)
            return product(blocks_ref[index, rows], rows_ref[near], 1)

        def add(index, value):
            x, y, _ = decode(list_ref[index], own_z)
            out_ref[x * NY + y if odd else y * NX + x, out_rows] += value

        for_groups(first, last, lambda index: copy(index, rows).wait(), compute, add)


def backward_kernel(place_ref, list_ref, source_ref, even_ref, odd_ref, *refs):
    outs, total_ref, blocks_ref, arrived, rows_ref, rows_arrived = refs[:5], *refs[5:]
    own_z, even_end, end = place_ref[0], place_ref[1], place_ref[2]

    def copy(index):
        return copy_block(list_ref[index], index, source_ref, blocks_ref, arrived)

    def copy_rows(index, source, place, source_rows, rows):
        return pltpu.make_async_copy(
            source.at[place, pl.ds(source_rows, rows.stop - rows.start)],
            rows_ref.at[index, pl.ds(rows.start, rows.stop - rows.start)],
            rows_arrived.at[index],
        )

    @pl.loop(0, even_end)
    def _(index):
        x, y, _ = decode(list_ref[index], own_z)
        copy(index).start()
        copy_rows(index, even_ref, y * NX + x, 0, slice(0, BLOCK)).start()

    @pl.loop(even_end, end)
    def _(index):
        x, y, _ = decode(list_ref[index], own_z)
        copy(index).start()
        copy_rows(index, even_ref, y * NX + x, BLOCK, slice(0, EXTRA_BACK)).start()
        copy_rows(index, odd_ref, x * NY + y, 0, slice(EXTRA_BACK, BLOCK)).start()

    total_ref[...] = jnp.zeros_like(total_ref)

    def wait(index):
        copy(index).wait()
        copy_rows(index, even_ref, 0, 0, slice(0, BLOCK)).wait()

    def compute(index):
        return product(blocks_ref[index], rows_ref[index], 0)

    def add(index, value):
        _, _, near = decode(list_ref[index], own_z)
        total_ref[near] += value

    for_groups(0, end, wait, compute, add)
    start = 0
    for out in outs:
        out[...] = total_ref[pl.ds(start, out.shape[0])]
        start += out.shape[0]


def call_kernel(body, place, entries, source, arrays, out_shapes, in_place=True):
    whole = pl.BlockSpec(memory_space=pltpu.VMEM)
    scalars = pl.BlockSpec(memory_space=pltpu.SMEM)
    anywhere = pl.BlockSpec(memory_space=pl.ANY)
    copies = [
        pltpu.VMEM((ENTRIES, BLOCK, BLOCK), jnp.float32),
        pltpu.SemaphoreType.DMA((ENTRIES,)),
    ]
    return pl.pallas_call(
        body,
        out_shape=[jax.ShapeDtypeStruct((*shape, HALF), jnp.float32) for shape in out_shapes],
        in_specs=[scalars, scalars, anywhere] + [whole if in_place else anywhere] * len(arrays),
        out_specs=[whole] * len(out_shapes),
        scratch_shapes=[pltpu.VMEM((2 * NZ, BLOCK, HALF), jnp.float32)]
        + copies * (1 if in_place else 2),
        compiler_params=pltpu.CompilerParams(vmem_limit_bytes=VMEM_LIMIT),
    )(place, entries, source, *arrays)


def halves_kernel(table_ref, out_ref):
    for index in range(out_ref.shape[0]):
        half = slice(index % 2 * HALF, (index % 2 + 1) * HALF)
        out_ref[index] = table_ref[:, half]


def repeat_halves(table):
    whole = pl.BlockSpec(memory_space=pltpu.VMEM)
    shape = jax.ShapeDtypeStruct((8, BLOCK, HALF), jnp.float32)
    return pl.pallas_call(halves_kernel, out_shape=shape, in_specs=[whole], out_specs=whole)(table)


def live_list(ids, own_x, own_z):
    numbers = jnp.arange(ENTRIES, dtype=jnp.int32)
    live = (ids >= 0) & (jnp.bitwise_and(ids, CB - 1) // NZ == own_x)
    odd = jnp.bitwise_and(ids // CB, 1) == 1
    even_live, odd_live = live & ~odd, live & odd
    before = numbers[None, :] < numbers[:, None]
    even_end = jnp.sum(even_live.astype(jnp.int32))
    rank = jnp.where(
        odd,
        even_end + jnp.sum((before & odd_live[None, :]).astype(jnp.int32), axis=1),
        jnp.sum((before & even_live[None, :]).astype(jnp.int32), axis=1),
    )
    hit = live[None, :] & (rank[None, :] == numbers[:, None])
    x = jnp.bitwise_and(own_x - numbers // (2 * SLOTS), NX - 1)
    gathered = x * (2 * SLOTS) + jnp.bitwise_and(numbers, 2 * SLOTS - 1)
    entries = jnp.sum(jnp.where(hit, (ids * ENTRIES + gathered)[None, :], 0), axis=1)
    return entries, jnp.stack([own_z, even_end, jnp.sum(live.astype(jnp.int32))])


def one_hot(indices, span_rows):
    return (indices[..., None] == jnp.arange(span_rows, dtype=jnp.int32)).astype(jnp.float32)


def per_device(table, blocks, block_ids, counts, users, positives, neg_index, popular):
    own_row = lax.axis_index("row")
    core = jnp.bitwise_and(lax.axis_index("col"), 1)
    own_z = jnp.bitwise_and(own_row, NZ - 1)
    source = lax.all_gather(blocks[0], BOTH, axis=0, tiled=True, axis_index_groups=X_CORE)

    far = exchange(repeat_halves(table), BOTH, Z_CORE)
    span_table = lax.dynamic_slice_in_dim(far, own_z // 4 * 2, 2)
    parts = [far, send_z(far, -1), send_z(far[:4], -2), send_z(far[4:], 2), send_z(far, 1)]
    live = jnp.arange(PAIRS, dtype=jnp.int32) < counts[0]
    marked = jnp.where(live, jnp.pad(block_ids[0], (0, PAIRS - SLOTS), constant_values=-1), -1)
    batch = jnp.take(positives[0], neg_index[0])
    picks = jnp.stack([users[0], positives[0], batch, popular[0], marked])
    other_picks = swap_cores(picks)
    is_first = core == 0
    span_picks = jnp.where(
        is_first, jnp.stack([picks, other_picks]), jnp.stack([other_picks, picks])
    )
    ids = span_picks[:, 4, :SLOTS]
    ids = jnp.stack([ids] + [send_x(ids, step) for step in range(1, NX)]).reshape(-1)
    entries, place = live_list(ids, own_row // NZ, own_z)
    source, span_picks, entries, place, *parts = lax.optimization_barrier(
        (source, span_picks, entries, place, *parts)
    )
    even, odd = (functools.partial(forward_kernel, odd) for odd in (False, True))
    (first,) = call_kernel(even, place, entries, source, parts, [(NX * NY, BLOCK + EXTRA)])
    entries, first = lax.optimization_barrier((entries, first))
    (second,) = call_kernel(odd, place, entries, source, parts, [(NX * NY, BLOCK - EXTRA)])

    first = lax.psum_scatter(
        first, "col", scatter_dimension=0, tiled=True, axis_index_groups=Y_GROUPS
    )
    second = second.reshape(NX, NY * (BLOCK - EXTRA), HALF)
    second = jnp.sum(exchange(second, "row", X_GROUPS), axis=0)
    second = exchange(second.reshape(NY, BLOCK - EXTRA, HALF), "col", Y_GROUPS)
    second = jnp.sum(second, axis=0)
    first = jnp.sum(exchange(first, "row", X_GROUPS), axis=0)
    current = jnp.concatenate([first, second]).reshape(2, BLOCK, HALF)

    final_rows = (span_table + current) / 2
    hot = one_hot(span_picks[:, :4], BLOCK)
    rows = jnp.einsum("hpij,hjd->hpid", hot, final_rows, precision=precise)
    user_rows, item_rows, batch_rows, popular_rows = (rows[:, i] for i in range(4))
    scores = jnp.stack(
        [
            jnp.sum(user_rows * item_rows, axis=-1),
            jnp.sum(user_rows * batch_rows, axis=-1),
            jnp.sum(user_rows * popular_rows, axis=-1),
        ],
        axis=1,
    )
    scores = scores + swap_cores(scores)
    first = scores[:, 1] - scores[:, 0]
    second = scores[:, 2] - scores[:, 0]
    losses = jax.nn.softplus(first) + jax.nn.softplus(second)
    span_losses = jnp.sum(losses, axis=1) / PAIRS
    span_loss = jnp.where(is_first, span_losses[0], span_losses[1]).reshape(1)
    pull_first = jax.nn.sigmoid(first)[..., None] / 2
    pull_second = jax.nn.sigmoid(second)[..., None] / 2
    pull_item = -(pull_first + pull_second)
    row_grads = jnp.stack(
        [
            pull_item * item_rows + pull_first * batch_rows + pull_second * popular_rows,
            pull_item * user_rows,
            pull_first * user_rows,
            pull_second * user_rows,
        ],
        axis=1,
    )
    scaled = jnp.einsum("hpij,hpid->hjd", hot, row_grads, precision=precise)

    all_rows = scaled.reshape(2 * BLOCK, HALF)
    first, second = all_rows[: BLOCK + EXTRA_BACK], all_rows[BLOCK + EXTRA_BACK :]
    first = exchange(jnp.broadcast_to(first[None], (NX, *first.shape)), "row", X_GROUPS)
    first = lax.all_gather(first, "col", axis=0, tiled=True, axis_index_groups=Y_GROUPS)
    second = exchange(jnp.broadcast_to(second[None], (NY, *second.shape)), "col", Y_GROUPS)
    second = second.reshape(NY * (BLOCK - EXTRA_BACK), HALF)
    second = exchange(jnp.broadcast_to(second[None], (NX, *second.shape)), "row", X_GROUPS)
    second = second.reshape(NX * NY, BLOCK - EXTRA_BACK, HALF)
    shapes = [(n, BLOCK) for n in (8, 8, 4, 4, 8)]
    own, after, two, two_far, before = call_kernel(
        backward_kernel, place, entries, source, [first, second], shapes, in_place=False
    )
    two = jnp.concatenate([send_z(two, 2), send_z(two_far, -2)])
    near = (own + send_z(after, 1) + send_z(before, -1) + two).reshape(4, 2, BLOCK, HALF)
    is_own = (jnp.arange(4) == own_z // 4)[:, None, None, None]
    near = near + jnp.where(is_own, scaled[None], 0.0)
    halves = exchange(near.reshape(8, BLOCK, HALF), BOTH, Z_CORE)
    halves = jnp.sum(halves.reshape(4, 2, BLOCK, HALF), axis=0)
    gradient = jnp.concatenate([halves[0], halves[1]], axis=1)
    return (gradient, span_loss)


def solution(mesh):
    in_specs = (
        P(("row", "col"), None),
        P(("row", "col"), None, None, None),
        P(("row", "col"), None),
        P(("row", "col")),
        P(("row", "col"), None),
        P(("row", "col"), None),
        P(("row", "col"), None),
        P(("row", "col"), None),
    )
    out_specs = (P(("row", "col"), None), P(("row", "col")))
    return jax.shard_map(
        per_device, mesh=mesh, in_specs=in_specs, out_specs=out_specs, check_vma=False
    )
```

```python
import functools

import jax
import jax.numpy as jnp
from jax import lax
from jax.experimental import pallas as pl
from jax.experimental.pallas import tpu as pltpu
from jax.sharding import PartitionSpec as P

BLOCK = 128
NX = 4
NZ = 16
NY = 8
HALF = 128
SLOTS = 16
CB = 64
PAIRS = 64
ENTRIES = 2 * NX * SLOTS
EXTRA = 32
EXTRA_BACK = 16
GROUP = 8
VMEM_LIMIT = 48 * 1024 * 1024

precise = lax.Precision.HIGHEST

BOTH = ("row", "col")
X_GROUPS = [[x * NZ + z for x in range(NX)] for z in range(NZ)]
Y_GROUPS = [[y * 2 + k for y in range(NY)] for k in range(2)]
X_CORE = [
    [(x * NZ + z) * 2 * NY + 2 * y + k for x in range(NX) for k in range(2)]
    for z in range(NZ)
    for y in range(NY)
]
Z_CORE = [
    [(x * NZ + 4 * a + b) * 2 * NY + 2 * y + k for a in range(4) for k in range(2)]
    for x in range(NX)
    for b in range(4)
    for y in range(NY)
]
CORE_SWAP = [(i, i ^ 1) for i in range(2 * NY)]


def send_x(values, step):
    pairs = [(x * NZ + z, ((x + step) % NX) * NZ + z) for x in range(NX) for z in range(NZ)]
    return lax.ppermute(values, "row", pairs)


def send_z(values, step):
    pairs = [(x * NZ + z, x * NZ + (z + step) % NZ) for x in range(NX) for z in range(NZ)]
    return lax.ppermute(values, "row", pairs)


def swap_cores(values):
    return lax.ppermute(values, "col", CORE_SWAP)


def exchange(values, axis, groups):
    return lax.all_to_all(
        values, axis, split_axis=0, concat_axis=0, tiled=True, axis_index_groups=groups
    )


def split_bf16(values):
    high = values.astype(jnp.bfloat16)
    low = (values - high.astype(jnp.float32)).astype(jnp.bfloat16)
    return high, low


def product(left, right, contract):
    left_high, left_low = split_bf16(left)
    right_high, right_low = split_bf16(right)
    rows = jnp.concatenate([left_high, left_low, left_high], axis=contract)
    columns = jnp.concatenate([right_high, right_high, right_low], axis=0)
    dims = (((contract,), (0,)), ((), ()))
    return lax.dot_general(rows, columns, dims, preferred_element_type=jnp.float32)


def copy_block(entry, place, source_ref, blocks_ref, arrived, rows=slice(0, BLOCK)):
    window = pl.ds(rows.start, rows.stop - rows.start)
    block = source_ref.at[jnp.bitwise_and(entry, ENTRIES - 1), window]
    return pltpu.make_async_copy(block, blocks_ref.at[place, window], arrived.at[place])


def decode(entry, own_z):
    number, position = jnp.bitwise_and(entry, ENTRIES - 1), entry // ENTRIES
    z = jnp.bitwise_and(position, NZ - 1)
    near = jnp.bitwise_and(z - own_z, 3) * 8 + (z // 4) * 2
    near = near + jnp.bitwise_and(number // SLOTS, 1)
    return number // (2 * SLOTS), position // (2 * CB), near


def for_groups(first, last, wait, compute, add):
    @pl.loop(0, (last - first + GROUP - 1) // GROUP)
    def _(step):
        start = first + GROUP * step
        wait(start)
        for index in range(1, GROUP):

            @pl.when(start + index < last)
            def _():
                wait(start + index)

        places = [jnp.minimum(start + index, last - 1) for index in range(GROUP)]
        values = [compute(place) for place in places]
        for index, (place, value) in enumerate(zip(places, values)):
            add(place, value if index == 0 else jnp.where(start + index < last, value, 0.0))


def forward_kernel(odd, place_ref, list_ref, source_ref, *refs):
    parts, out_ref, rows_ref, blocks_ref, arrived = refs[:5], refs[5], refs[6], refs[7], refs[8]
    own_z, even_end, end = place_ref[0], place_ref[1], place_ref[2]

    def copy(index, rows):
        return copy_block(list_ref[index], index, source_ref, blocks_ref, arrived, rows)

    top, rest, whole = slice(0, EXTRA), slice(EXTRA, BLOCK), slice(0, BLOCK)
    if odd:
        spans = [(even_end, end, rest, slice(0, BLOCK - EXTRA))]
    else:
        spans = [(0, even_end, whole, whole), (even_end, end, top, slice(BLOCK, BLOCK + EXTRA))]
    for first, last, rows, _ in spans:

        @pl.loop(first, last)
        def _(index):
            copy(index, rows).start()

    out_ref[...] = jnp.zeros_like(out_ref)
    start = 0
    for part in parts:
        rows_ref[pl.ds(start, part.shape[0])] = part[...]
        start += part.shape[0]

    for first, last, rows, out_rows in spans:

        def compute(index):
            _, _, near = decode(list_ref[index], own_z)
            return product(blocks_ref[index, rows], rows_ref[near], 1)

        def add(index, value):
            x, y, _ = decode(list_ref[index], own_z)
            out_ref[x * NY + y if odd else y * NX + x, out_rows] += value

        for_groups(first, last, lambda index: copy(index, rows).wait(), compute, add)


def backward_kernel(place_ref, list_ref, source_ref, even_ref, odd_ref, *refs):
    outs, total_ref, blocks_ref, arrived, rows_ref, rows_arrived = refs[:5], *refs[5:]
    own_z, even_end, end = place_ref[0], place_ref[1], place_ref[2]

    def copy(index):
        return copy_block(list_ref[index], index, source_ref, blocks_ref, arrived)

    def copy_rows(index, source, place, source_rows, rows):
        return pltpu.make_async_copy(
            source.at[place, pl.ds(source_rows, rows.stop - rows.start)],
            rows_ref.at[index, pl.ds(rows.start, rows.stop - rows.start)],
            rows_arrived.at[index],
        )

    @pl.loop(0, even_end)
    def _(index):
        x, y, _ = decode(list_ref[index], own_z)
        copy(index).start()
        copy_rows(index, even_ref, y * NX + x, 0, slice(0, BLOCK)).start()

    @pl.loop(even_end, end)
    def _(index):
        x, y, _ = decode(list_ref[index], own_z)
        copy(index).start()
        copy_rows(index, even_ref, y * NX + x, BLOCK, slice(0, EXTRA_BACK)).start()
        copy_rows(index, odd_ref, x * NY + y, 0, slice(EXTRA_BACK, BLOCK)).start()

    total_ref[...] = jnp.zeros_like(total_ref)

    def wait(index):
        copy(index).wait()
        copy_rows(index, even_ref, 0, 0, slice(0, BLOCK)).wait()

    def compute(index):
        return product(blocks_ref[index], rows_ref[index], 0)

    def add(index, value):
        _, _, near = decode(list_ref[index], own_z)
        total_ref[near] += value

    for_groups(0, end, wait, compute, add)
    start = 0
    for out in outs:
        out[...] = total_ref[pl.ds(start, out.shape[0])]
        start += out.shape[0]


def call_kernel(body, place, entries, source, arrays, out_shapes, in_place=True):
    whole = pl.BlockSpec(memory_space=pltpu.VMEM)
    scalars = pl.BlockSpec(memory_space=pltpu.SMEM)
    anywhere = pl.BlockSpec(memory_space=pl.ANY)
    copies = [
        pltpu.VMEM((ENTRIES, BLOCK, BLOCK), jnp.float32),
        pltpu.SemaphoreType.DMA((ENTRIES,)),
    ]
    return pl.pallas_call(
        body,
        out_shape=[jax.ShapeDtypeStruct((*shape, HALF), jnp.float32) for shape in out_shapes],
        in_specs=[scalars, scalars, anywhere] + [whole if in_place else anywhere] * len(arrays),
        out_specs=[whole] * len(out_shapes),
        scratch_shapes=[pltpu.VMEM((2 * NZ, BLOCK, HALF), jnp.float32)]
        + copies * (1 if in_place else 2),
        compiler_params=pltpu.CompilerParams(vmem_limit_bytes=VMEM_LIMIT),
    )(place, entries, source, *arrays)


def halves_kernel(table_ref, out_ref):
    for index in range(out_ref.shape[0]):
        half = slice(index % 2 * HALF, (index % 2 + 1) * HALF)
        out_ref[index] = table_ref[:, half]


def repeat_halves(table):
    whole = pl.BlockSpec(memory_space=pltpu.VMEM)
    shape = jax.ShapeDtypeStruct((8, BLOCK, HALF), jnp.float32)
    return pl.pallas_call(halves_kernel, out_shape=shape, in_specs=[whole], out_specs=whole)(table)


def live_list(ids, own_x, own_z):
    numbers = jnp.arange(ENTRIES, dtype=jnp.int32)
    live = (ids >= 0) & (jnp.bitwise_and(ids, CB - 1) // NZ == own_x)
    odd = jnp.bitwise_and(ids // CB, 1) == 1
    even_live, odd_live = live & ~odd, live & odd
    before = numbers[None, :] < numbers[:, None]
    even_end = jnp.sum(even_live.astype(jnp.int32))
    rank = jnp.where(
        odd,
        even_end + jnp.sum((before & odd_live[None, :]).astype(jnp.int32), axis=1),
        jnp.sum((before & even_live[None, :]).astype(jnp.int32), axis=1),
    )
    hit = live[None, :] & (rank[None, :] == numbers[:, None])
    x = jnp.bitwise_and(own_x - numbers // (2 * SLOTS), NX - 1)
    gathered = x * (2 * SLOTS) + jnp.bitwise_and(numbers, 2 * SLOTS - 1)
    entries = jnp.sum(jnp.where(hit, (ids * ENTRIES + gathered)[None, :], 0), axis=1)
    return entries, jnp.stack([own_z, even_end, jnp.sum(live.astype(jnp.int32))])


def one_hot(indices, span_rows):
    return (indices[..., None] == jnp.arange(span_rows, dtype=jnp.int32)).astype(jnp.float32)


def per_device(table, blocks, block_ids, counts, users, positives, neg_index, popular):
    own_row = lax.axis_index("row")
    core = jnp.bitwise_and(lax.axis_index("col"), 1)
    own_z = jnp.bitwise_and(own_row, NZ - 1)
    source = lax.all_gather(blocks[0], BOTH, axis=0, tiled=True, axis_index_groups=X_CORE)

    far = exchange(repeat_halves(table), BOTH, Z_CORE)
    span_table = lax.dynamic_slice_in_dim(far, own_z // 4 * 2, 2)
    parts = [far, send_z(far, -1), send_z(far[:4], -2), send_z(far[4:], 2), send_z(far, 1)]
    live = jnp.arange(PAIRS, dtype=jnp.int32) < counts[0]
    marked = jnp.where(live, jnp.pad(block_ids[0], (0, PAIRS - SLOTS), constant_values=-1), -1)
    batch = jnp.take(positives[0], neg_index[0])
    picks = jnp.stack([users[0], positives[0], batch, popular[0], marked])
    other_picks = swap_cores(picks)
    is_first = core == 0
    span_picks = jnp.where(
        is_first, jnp.stack([picks, other_picks]), jnp.stack([other_picks, picks])
    )
    ids = span_picks[:, 4, :SLOTS]
    ids = jnp.stack([ids] + [send_x(ids, step) for step in range(1, NX)]).reshape(-1)
    entries, place = live_list(ids, own_row // NZ, own_z)
    source, span_picks, entries, place, *parts = lax.optimization_barrier(
        (source, span_picks, entries, place, *parts)
    )
    even, odd = (functools.partial(forward_kernel, odd) for odd in (False, True))
    (first,) = call_kernel(even, place, entries, source, parts, [(NX * NY, BLOCK + EXTRA)])
    entries, first = lax.optimization_barrier((entries, first))
    (second,) = call_kernel(odd, place, entries, source, parts, [(NX * NY, BLOCK - EXTRA)])

    first = lax.psum_scatter(
        first, "col", scatter_dimension=0, tiled=True, axis_index_groups=Y_GROUPS
    )
    second = second.reshape(NX, NY * (BLOCK - EXTRA), HALF)
    second = jnp.sum(exchange(second, "row", X_GROUPS), axis=0)
    second = exchange(second.reshape(NY, BLOCK - EXTRA, HALF), "col", Y_GROUPS)
    second = jnp.sum(second, axis=0)
    first = jnp.sum(exchange(first, "row", X_GROUPS), axis=0)
    current = jnp.concatenate([first, second]).reshape(2, BLOCK, HALF)

    final_rows = (span_table + current) / 2
    hot = one_hot(span_picks[:, :4], BLOCK)
    rows = jnp.einsum("hpij,hjd->hpid", hot, final_rows, precision=precise)
    user_rows, item_rows, batch_rows, popular_rows = (rows[:, i] for i in range(4))
    scores = jnp.stack(
        [
            jnp.sum(user_rows * item_rows, axis=-1),
            jnp.sum(user_rows * batch_rows, axis=-1),
            jnp.sum(user_rows * popular_rows, axis=-1),
        ],
        axis=1,
    )
    scores = scores + swap_cores(scores)
    first = scores[:, 1] - scores[:, 0]
    second = scores[:, 2] - scores[:, 0]
    losses = jax.nn.softplus(first) + jax.nn.softplus(second)
    span_losses = jnp.sum(losses, axis=1) / PAIRS
    span_loss = jnp.where(is_first, span_losses[0], span_losses[1]).reshape(1)
    pull_first = jax.nn.sigmoid(first)[..., None] / 2
    pull_second = jax.nn.sigmoid(second)[..., None] / 2
    pull_item = -(pull_first + pull_second)
    row_grads = jnp.stack(
        [
            pull_item * item_rows + pull_first * batch_rows + pull_second * popular_rows,
            pull_item * user_rows,
            pull_first * user_rows,
            pull_second * user_rows,
        ],
        axis=1,
    )
    scaled = jnp.einsum("hpij,hpid->hjd", hot, row_grads, precision=precise)

    all_rows = scaled.reshape(2 * BLOCK, HALF)
    first, second = all_rows[: BLOCK + EXTRA_BACK], all_rows[BLOCK + EXTRA_BACK :]
    first = exchange(jnp.broadcast_to(first[None], (NX, *first.shape)), "row", X_GROUPS)
    first = lax.all_gather(first, "col", axis=0, tiled=True, axis_index_groups=Y_GROUPS)
    second = exchange(jnp.broadcast_to(second[None], (NY, *second.shape)), "col", Y_GROUPS)
    second = second.reshape(NY * (BLOCK - EXTRA_BACK), HALF)
    second = exchange(jnp.broadcast_to(second[None], (NX, *second.shape)), "row", X_GROUPS)
    second = second.reshape(NX * NY, BLOCK - EXTRA_BACK, HALF)
    shapes = [(n, BLOCK) for n in (8, 8, 4, 4, 8)]
    own, after, two, two_far, before = call_kernel(
        backward_kernel, place, entries, source, [first, second], shapes, in_place=False
    )
    two = jnp.concatenate([send_z(two, 2), send_z(two_far, -2)])
    near = (own + send_z(after, 1) + send_z(before, -1) + two).reshape(4, 2, BLOCK, HALF)
    at_stride = [
        lax.dynamic_index_in_dim(near, jnp.bitwise_and(own_z // 4 + m, 3), keepdims=False)
        for m in range(4)
    ]
    halves = scaled + at_stride[0] + send_z(at_stride[2], 8)
    halves = halves + send_z(at_stride[1], 4) + send_z(at_stride[3], -4)
    own_half = jnp.where(is_first, halves[0], halves[1])
    other_half = swap_cores(jnp.where(is_first, halves[1], halves[0]))
    gradient = jnp.concatenate(
        [jnp.where(is_first, own_half, other_half), jnp.where(is_first, other_half, own_half)], axis=1
    )
    return (gradient, span_loss)


def solution(mesh):
    in_specs = (
        P(("row", "col"), None),
        P(("row", "col"), None, None, None),
        P(("row", "col"), None),
        P(("row", "col")),
        P(("row", "col"), None),
        P(("row", "col"), None),
        P(("row", "col"), None),
        P(("row", "col"), None),
    )
    out_specs = (P(("row", "col"), None), P(("row", "col")))
    return jax.shard_map(
        per_device, mesh=mesh, in_specs=in_specs, out_specs=out_specs, check_vma=False
    )
```

```python
import functools

import jax
import jax.numpy as jnp
from jax import lax
from jax.experimental import pallas as pl
from jax.experimental.pallas import tpu as pltpu
from jax.sharding import PartitionSpec as P

BLOCK = 128
NX = 4
NZ = 16
NY = 8
HALF = 128
SLOTS = 16
CB = 64
PAIRS = 64
ENTRIES = 2 * NX * SLOTS
EXTRA = 16
EXTRA_BACK = 16
GROUP = 8
VMEM_LIMIT = 48 * 1024 * 1024

precise = lax.Precision.HIGHEST

BOTH = ("row", "col")
X_GROUPS = [[x * NZ + z for x in range(NX)] for z in range(NZ)]
Y_GROUPS = [[y * 2 + k for y in range(NY)] for k in range(2)]
X_CORE = [
    [(x * NZ + z) * 2 * NY + 2 * y + k for x in range(NX) for k in range(2)]
    for z in range(NZ)
    for y in range(NY)
]
Z_CORE = [
    [(x * NZ + 4 * a + b) * 2 * NY + 2 * y + k for a in range(4) for k in range(2)]
    for x in range(NX)
    for b in range(4)
    for y in range(NY)
]
CORE_SWAP = [(i, i ^ 1) for i in range(2 * NY)]


def send_x(values, step):
    pairs = [(x * NZ + z, ((x + step) % NX) * NZ + z) for x in range(NX) for z in range(NZ)]
    return lax.ppermute(values, "row", pairs)


def send_z(values, step):
    pairs = [(x * NZ + z, x * NZ + (z + step) % NZ) for x in range(NX) for z in range(NZ)]
    return lax.ppermute(values, "row", pairs)


def swap_cores(values):
    return lax.ppermute(values, "col", CORE_SWAP)


def exchange(values, axis, groups):
    return lax.all_to_all(
        values, axis, split_axis=0, concat_axis=0, tiled=True, axis_index_groups=groups
    )


def split_bf16(values):
    high = values.astype(jnp.bfloat16)
    low = (values - high.astype(jnp.float32)).astype(jnp.bfloat16)
    return high, low


def product(left, right, contract):
    left_high, left_low = split_bf16(left)
    right_high, right_low = split_bf16(right)
    rows = jnp.concatenate([left_high, left_low, left_high], axis=contract)
    columns = jnp.concatenate([right_high, right_high, right_low], axis=0)
    dims = (((contract,), (0,)), ((), ()))
    return lax.dot_general(rows, columns, dims, preferred_element_type=jnp.float32)


def copy_block(entry, place, source_ref, blocks_ref, arrived, rows=slice(0, BLOCK)):
    window = pl.ds(rows.start, rows.stop - rows.start)
    block = source_ref.at[jnp.bitwise_and(entry, ENTRIES - 1), window]
    return pltpu.make_async_copy(block, blocks_ref.at[place, window], arrived.at[place])


def decode(entry, own_z):
    number, position = jnp.bitwise_and(entry, ENTRIES - 1), entry // ENTRIES
    z = jnp.bitwise_and(position, NZ - 1)
    near = jnp.bitwise_and(z - own_z, 3) * 8 + (z // 4) * 2
    near = near + jnp.bitwise_and(number // SLOTS, 1)
    return number // (2 * SLOTS), position // (2 * CB), near


def for_groups(first, last, wait, compute, add):
    @pl.loop(0, (last - first + GROUP - 1) // GROUP)
    def _(step):
        start = first + GROUP * step
        wait(start)
        for index in range(1, GROUP):

            @pl.when(start + index < last)
            def _():
                wait(start + index)

        places = [jnp.minimum(start + index, last - 1) for index in range(GROUP)]
        values = [compute(place) for place in places]
        for index, (place, value) in enumerate(zip(places, values)):
            add(place, value if index == 0 else jnp.where(start + index < last, value, 0.0))


def forward_kernel(odd, place_ref, list_ref, source_ref, *refs):
    parts, out_ref, rows_ref, blocks_ref, arrived = refs[:5], refs[5], refs[6], refs[7], refs[8]
    own_z, even_end, end = place_ref[0], place_ref[1], place_ref[2]

    def copy(index, rows):
        return copy_block(list_ref[index], index, source_ref, blocks_ref, arrived, rows)

    top, rest, whole = slice(0, EXTRA), slice(EXTRA, BLOCK), slice(0, BLOCK)
    if odd:
        spans = [(even_end, end, rest, slice(0, BLOCK - EXTRA))]
    else:
        spans = [(0, even_end, whole, whole), (even_end, end, top, slice(BLOCK, BLOCK + EXTRA))]
    for first, last, rows, _ in spans:

        @pl.loop(first, last)
        def _(index):
            copy(index, rows).start()

    out_ref[...] = jnp.zeros_like(out_ref)
    start = 0
    for part in parts:
        rows_ref[pl.ds(start, part.shape[0])] = part[...]
        start += part.shape[0]

    for first, last, rows, out_rows in spans:

        def compute(index):
            _, _, near = decode(list_ref[index], own_z)
            return product(blocks_ref[index, rows], rows_ref[near], 1)

        def add(index, value):
            x, y, _ = decode(list_ref[index], own_z)
            out_ref[x * NY + y if odd else y * NX + x, out_rows] += value

        for_groups(first, last, lambda index: copy(index, rows).wait(), compute, add)


def backward_kernel(place_ref, list_ref, source_ref, even_ref, odd_ref, *refs):
    outs, total_ref, blocks_ref, arrived, rows_ref, rows_arrived = refs[:5], *refs[5:]
    own_z, even_end, end = place_ref[0], place_ref[1], place_ref[2]

    def copy(index):
        return copy_block(list_ref[index], index, source_ref, blocks_ref, arrived)

    def copy_rows(index, source, place, source_rows, rows):
        return pltpu.make_async_copy(
            source.at[place, pl.ds(source_rows, rows.stop - rows.start)],
            rows_ref.at[index, pl.ds(rows.start, rows.stop - rows.start)],
            rows_arrived.at[index],
        )

    @pl.loop(0, even_end)
    def _(index):
        x, y, _ = decode(list_ref[index], own_z)
        copy(index).start()
        copy_rows(index, even_ref, y * NX + x, 0, slice(0, BLOCK)).start()

    @pl.loop(even_end, end)
    def _(index):
        x, y, _ = decode(list_ref[index], own_z)
        copy(index).start()
        copy_rows(index, even_ref, y * NX + x, BLOCK, slice(0, EXTRA_BACK)).start()
        copy_rows(index, odd_ref, x * NY + y, 0, slice(EXTRA_BACK, BLOCK)).start()

    total_ref[...] = jnp.zeros_like(total_ref)

    def wait(index):
        copy(index).wait()
        copy_rows(index, even_ref, 0, 0, slice(0, BLOCK)).wait()

    def compute(index):
        return product(blocks_ref[index], rows_ref[index], 0)

    def add(index, value):
        _, _, near = decode(list_ref[index], own_z)
        total_ref[near] += value

    for_groups(0, end, wait, compute, add)
    start = 0
    for out in outs:
        out[...] = total_ref[pl.ds(start, out.shape[0])]
        start += out.shape[0]


def call_kernel(body, place, entries, source, arrays, out_shapes, in_place=True):
    whole = pl.BlockSpec(memory_space=pltpu.VMEM)
    scalars = pl.BlockSpec(memory_space=pltpu.SMEM)
    anywhere = pl.BlockSpec(memory_space=pl.ANY)
    copies = [
        pltpu.VMEM((ENTRIES, BLOCK, BLOCK), jnp.float32),
        pltpu.SemaphoreType.DMA((ENTRIES,)),
    ]
    return pl.pallas_call(
        body,
        out_shape=[jax.ShapeDtypeStruct((*shape, HALF), jnp.float32) for shape in out_shapes],
        in_specs=[scalars, scalars, anywhere] + [whole if in_place else anywhere] * len(arrays),
        out_specs=[whole] * len(out_shapes),
        scratch_shapes=[pltpu.VMEM((2 * NZ, BLOCK, HALF), jnp.float32)]
        + copies * (1 if in_place else 2),
        compiler_params=pltpu.CompilerParams(vmem_limit_bytes=VMEM_LIMIT),
    )(place, entries, source, *arrays)


def halves_kernel(table_ref, out_ref):
    for index in range(out_ref.shape[0]):
        half = slice(index % 2 * HALF, (index % 2 + 1) * HALF)
        out_ref[index] = table_ref[:, half]


def repeat_halves(table):
    whole = pl.BlockSpec(memory_space=pltpu.VMEM)
    shape = jax.ShapeDtypeStruct((8, BLOCK, HALF), jnp.float32)
    return pl.pallas_call(halves_kernel, out_shape=shape, in_specs=[whole], out_specs=whole)(table)


def live_list(ids, own_x, own_z):
    numbers = jnp.arange(ENTRIES, dtype=jnp.int32)
    live = (ids >= 0) & (jnp.bitwise_and(ids, CB - 1) // NZ == own_x)
    odd = jnp.bitwise_and(ids // CB, 1) == 1
    even_live, odd_live = live & ~odd, live & odd
    before = numbers[None, :] < numbers[:, None]
    even_end = jnp.sum(even_live.astype(jnp.int32))
    rank = jnp.where(
        odd,
        even_end + jnp.sum((before & odd_live[None, :]).astype(jnp.int32), axis=1),
        jnp.sum((before & even_live[None, :]).astype(jnp.int32), axis=1),
    )
    hit = live[None, :] & (rank[None, :] == numbers[:, None])
    x = jnp.bitwise_and(own_x - numbers // (2 * SLOTS), NX - 1)
    gathered = x * (2 * SLOTS) + jnp.bitwise_and(numbers, 2 * SLOTS - 1)
    entries = jnp.sum(jnp.where(hit, (ids * ENTRIES + gathered)[None, :], 0), axis=1)
    return entries, jnp.stack([own_z, even_end, jnp.sum(live.astype(jnp.int32))])


def one_hot(indices, span_rows):
    return (indices[..., None] == jnp.arange(span_rows, dtype=jnp.int32)).astype(jnp.float32)


def per_device(table, blocks, block_ids, counts, users, positives, neg_index, popular):
    own_row = lax.axis_index("row")
    core = jnp.bitwise_and(lax.axis_index("col"), 1)
    own_z = jnp.bitwise_and(own_row, NZ - 1)
    source = lax.all_gather(blocks[0], BOTH, axis=0, tiled=True, axis_index_groups=X_CORE)

    far = exchange(repeat_halves(table), BOTH, Z_CORE)
    span_table = lax.dynamic_slice_in_dim(far, own_z // 4 * 2, 2)
    parts = [far, send_z(far, -1), send_z(far[:4], -2), send_z(far[4:], 2), send_z(far, 1)]
    live = jnp.arange(PAIRS, dtype=jnp.int32) < counts[0]
    marked = jnp.where(live, jnp.pad(block_ids[0], (0, PAIRS - SLOTS), constant_values=-1), -1)
    batch = jnp.take(positives[0], neg_index[0])
    picks = jnp.stack([users[0], positives[0], batch, popular[0], marked])
    other_picks = swap_cores(picks)
    is_first = core == 0
    span_picks = jnp.where(
        is_first, jnp.stack([picks, other_picks]), jnp.stack([other_picks, picks])
    )
    ids = span_picks[:, 4, :SLOTS]
    ids = jnp.stack([ids] + [send_x(ids, step) for step in range(1, NX)]).reshape(-1)
    entries, place = live_list(ids, own_row // NZ, own_z)
    source, span_picks, entries, place, *parts = lax.optimization_barrier(
        (source, span_picks, entries, place, *parts)
    )
    even, odd = (functools.partial(forward_kernel, odd) for odd in (False, True))
    (first,) = call_kernel(even, place, entries, source, parts, [(NX * NY, BLOCK + EXTRA)])
    entries, first = lax.optimization_barrier((entries, first))
    (second,) = call_kernel(odd, place, entries, source, parts, [(NX * NY, BLOCK - EXTRA)])

    first = lax.psum_scatter(
        first, "col", scatter_dimension=0, tiled=True, axis_index_groups=Y_GROUPS
    )
    second = second.reshape(NX, NY * (BLOCK - EXTRA), HALF)
    second = jnp.sum(exchange(second, "row", X_GROUPS), axis=0)
    second = exchange(second.reshape(NY, BLOCK - EXTRA, HALF), "col", Y_GROUPS)
    second = jnp.sum(second, axis=0)
    first = jnp.sum(exchange(first, "row", X_GROUPS), axis=0)
    current = jnp.concatenate([first, second]).reshape(2, BLOCK, HALF)

    final_rows = (span_table + current) / 2
    hot = one_hot(span_picks[:, :4], BLOCK)
    rows = jnp.einsum("hpij,hjd->hpid", hot, final_rows, precision=precise)
    user_rows, item_rows, batch_rows, popular_rows = (rows[:, i] for i in range(4))
    scores = jnp.stack(
        [
            jnp.sum(user_rows * item_rows, axis=-1),
            jnp.sum(user_rows * batch_rows, axis=-1),
            jnp.sum(user_rows * popular_rows, axis=-1),
        ],
        axis=1,
    )
    scores = scores + swap_cores(scores)
    first = scores[:, 1] - scores[:, 0]
    second = scores[:, 2] - scores[:, 0]
    losses = jax.nn.softplus(first) + jax.nn.softplus(second)
    span_losses = jnp.sum(losses, axis=1) / PAIRS
    span_loss = jnp.where(is_first, span_losses[0], span_losses[1]).reshape(1)
    pull_first = jax.nn.sigmoid(first)[..., None] / 2
    pull_second = jax.nn.sigmoid(second)[..., None] / 2
    pull_item = -(pull_first + pull_second)
    row_grads = jnp.stack(
        [
            pull_item * item_rows + pull_first * batch_rows + pull_second * popular_rows,
            pull_item * user_rows,
            pull_first * user_rows,
            pull_second * user_rows,
        ],
        axis=1,
    )
    scaled = jnp.einsum("hpij,hpid->hjd", hot, row_grads, precision=precise)

    all_rows = scaled.reshape(2 * BLOCK, HALF)
    first, second = all_rows[: BLOCK + EXTRA_BACK], all_rows[BLOCK + EXTRA_BACK :]
    first = exchange(jnp.broadcast_to(first[None], (NX, *first.shape)), "row", X_GROUPS)
    first = lax.all_gather(first, "col", axis=0, tiled=True, axis_index_groups=Y_GROUPS)
    second = exchange(jnp.broadcast_to(second[None], (NY, *second.shape)), "col", Y_GROUPS)
    second = second.reshape(NY * (BLOCK - EXTRA_BACK), HALF)
    second = exchange(jnp.broadcast_to(second[None], (NX, *second.shape)), "row", X_GROUPS)
    second = second.reshape(NX * NY, BLOCK - EXTRA_BACK, HALF)
    shapes = [(n, BLOCK) for n in (8, 8, 4, 4, 8)]
    own, after, two, two_far, before = call_kernel(
        backward_kernel, place, entries, source, [first, second], shapes, in_place=False
    )
    two = jnp.concatenate([send_z(two, 2), send_z(two_far, -2)])
    near = (own + send_z(after, 1) + send_z(before, -1) + two).reshape(4, 2, BLOCK, HALF)
    at_stride = [
        lax.dynamic_index_in_dim(near, jnp.bitwise_and(own_z // 4 + m, 3), keepdims=False)
        for m in range(4)
    ]
    halves = scaled + at_stride[0] + send_z(at_stride[2], 8)
    halves = halves + send_z(at_stride[1], 4) + send_z(at_stride[3], -4)
    own_half = jnp.where(is_first, halves[0], halves[1])
    other_half = swap_cores(jnp.where(is_first, halves[1], halves[0]))
    gradient = jnp.concatenate(
        [jnp.where(is_first, own_half, other_half), jnp.where(is_first, other_half, own_half)], axis=1
    )
    return (gradient, span_loss)


def solution(mesh):
    in_specs = (
        P(("row", "col"), None),
        P(("row", "col"), None, None, None),
        P(("row", "col"), None),
        P(("row", "col")),
        P(("row", "col"), None),
        P(("row", "col"), None),
        P(("row", "col"), None),
        P(("row", "col"), None),
    )
    out_specs = (P(("row", "col"), None), P(("row", "col")))
    return jax.shard_map(
        per_device, mesh=mesh, in_specs=in_specs, out_specs=out_specs, check_vma=False
    )
```
